256 devices in a mesh: dp: 64 (over z, y, core), mp: 4 (over x).
Axes of the slice: x: 4, y: 4, z: 8, core: 2. Of those that a mesh axis runs over, the one named last changes fastest.
Arguments:
- left_factors: bfloat16 [128, 5, 16, 32, 1024], P('dp', None, 'mp'), may hold values from -1 to 1
- right_factors: bfloat16 [128, 5, 16, 32, 1024], P('dp', None, 'mp'), may hold values from -0.1875 to 0.1875
- observations: bfloat16 [128, 5, 64, 1024], P('dp'), may hold values from -40 to 40
Outputs:
- solution: float32 [16, 64, 1024], P('mp')
- direction: float32 [16, 64, 1024], P('mp')
- residual_estimate: float32 [64], replicated
The draws below stay inside these ranges and needn't reach their ends.
All inputs are finite; a program needn't handle non-finite values.
Results may differ from the reference program's by a relative error of at most 0.035.
Values may be sent and summed in bfloat16 or wider, within the bound.
No kernel may reach another device: no remote copies, remote signals or barrier semaphores. Data moves between devices by JAX's collectives and lax.ppermute only.
A program may use at most 64 MiB of HBM per device.

```python
import math
import jax
import jax.numpy as jnp
from jax import lax

TILE = 1024
RANK = 32
COMP = 5
SOLVES = 64
ITERS = 2
ROW_TILES = 128
COL_TILES = 16


def draw_observations(key, part):
    key = jax.random.fold_in(key, 7)
    first, second = jax.random.split(key, 2)
    shape = (ROW_TILES, COMP, SOLVES, TILE)
    rise = 1.0 + 2.0 * jnp.arange(ROW_TILES, dtype=jnp.float32)[:, None, None, None] / max(ROW_TILES - 1, 1)
    spread = jnp.exp(jax.random.uniform(second, (ROW_TILES, COMP, 1, TILE), minval=0.0, maxval=math.log(10.0)))
    values = jax.random.normal(first, shape) * rise * spread
    return jnp.clip(values, -40.0, 40.0).astype(jnp.bfloat16)


def levels(rng, shape, cuts, least, largest):
    loudness = 1.0
    for axis_at, parts in cuts:
        heights = jax.random.uniform(jax.random.fold_in(jax.random.fold_in(rng, 6), axis_at), (parts,), jnp.float32, least / len(cuts), largest / len(cuts))
        loudness = loudness * jnp.repeat(jnp.exp(heights), shape[axis_at] // parts).reshape((-1,) + (1,) * (len(shape) - 1 - axis_at))
    return loudness


def gaussian(rng, extent, scale, bound, cuts=(), held_as=jnp.bfloat16):
    factor_of = levels(rng, extent, cuts, -0.22, 0.18) if cuts else 1.0
    entries = jax.random.normal(rng, extent, jnp.float32) * scale * factor_of
    return jnp.minimum(jnp.maximum(entries, -bound), bound).astype(held_as)


def setup_inputs(seed: int = 0) -> dict:
    arg_keys = jax.random.split(jax.random.key(seed), 4)
    return {
        "left_factors": gaussian(arg_keys[0], (ROW_TILES, COMP, COL_TILES, RANK, TILE), RANK ** -0.5, 1.0, ((0, 64), (2, 4))),
        "right_factors": gaussian(arg_keys[1], (ROW_TILES, COMP, COL_TILES, RANK, TILE), TILE ** -0.5, 0.1875, ((0, 64), (2, 4))),
        "observations": draw_observations(jax.random.fold_in(arg_keys[3], 71), 0),
    }


EPSILON = 1e-06

def round_half(values):
    return lax.optimization_barrier(values.astype(jnp.bfloat16)).astype(jnp.float32)

def apply_forward(left_factors, right_factors, model):
    model_half = round_half(model)

    def one_tile_row(pair):
        left_row, right_row = pair
        coeffs = jnp.einsum('ctkb,tnb->ctkn', right_row.astype(jnp.float32), model_half, precision=lax.Precision.HIGHEST)
        coeffs = round_half(coeffs)
        return jnp.einsum('ctkb,ctkn->cnb', left_row.astype(jnp.float32), coeffs, precision=lax.Precision.HIGHEST)
    return lax.map(one_tile_row, (left_factors, right_factors))

def apply_backward(left_factors, right_factors, data_field):

    def step(total, triple):
        left_row, right_row, data_row = triple
        coeffs = jnp.einsum('ctkb,cnb->ctkn', left_row.astype(jnp.float32), round_half(data_row), precision=lax.Precision.HIGHEST)
        coeffs = round_half(coeffs)
        return (total + jnp.einsum('ctkb,ctkn->tnb', right_row.astype(jnp.float32), coeffs, precision=lax.Precision.HIGHEST), None)
    start = jnp.zeros((COL_TILES, SOLVES, TILE), jnp.float32)
    total, unused = lax.scan(step, start, (left_factors, right_factors, data_field))
    return total

def reference(left_factors, right_factors, observations):
    values = observations.astype(jnp.float32)
    data_len = jnp.sqrt(lax.optimization_barrier(jnp.sum(values * values, axis=(0, 1, 3))) + EPSILON)
    data_unit = values / data_len[:, None]
    model_raw = apply_backward(left_factors, right_factors, data_unit)
    model_len = jnp.sqrt(lax.optimization_barrier(jnp.sum(model_raw * model_raw, axis=(0, 2))) + EPSILON)
    model = model_raw / model_len[:, None]
    solution = jnp.zeros_like(model)
    direction = model
    residual_estimate = data_len
    diagonal_bar = model_len
    for sweep in range(ITERS):
        data_raw = apply_forward(left_factors, right_factors, model) - model_len[:, None] * data_unit
        data_len = jnp.sqrt(lax.optimization_barrier(jnp.sum(data_raw * data_raw, axis=(0, 1, 3))) + EPSILON)
        data_unit = data_raw / data_len[:, None]
        model_raw = apply_backward(left_factors, right_factors, data_unit) - data_len[:, None] * model
        model_len = jnp.sqrt(lax.optimization_barrier(jnp.sum(model_raw * model_raw, axis=(0, 2))) + EPSILON)
        model = model_raw / model_len[:, None]
        rotation = jnp.sqrt(diagonal_bar * diagonal_bar + data_len * data_len)
        cosine_term = diagonal_bar / rotation
        sine_term = data_len / rotation
        coupling = sine_term * model_len
        diagonal_bar = -cosine_term * model_len
        step_size = cosine_term * residual_estimate
        residual_estimate = sine_term * residual_estimate
        solution = solution + (step_size / rotation)[:, None] * direction
        direction = model - (coupling / rotation)[:, None] * direction
    return (solution, direction, residual_estimate)
```

```python
import jax
import jax.numpy as jnp
from jax import lax
from jax.sharding import Mesh
from jax.sharding import PartitionSpec as P

ITERS = 2
EPSILON = 1e-06
ORDER = (2, 1, 0, 5, 4, 3, 8, 7, 6, 9)
BF = jnp.bfloat16
F32 = jnp.float32


def pieces(values):
    first = lax.reduce_precision(values, 8, 7)
    rest = values - first
    second = lax.reduce_precision(rest, 8, 7)
    third = lax.reduce_precision(rest - second, 8, 7)
    return jnp.stack([first, second, third], axis=-1)


def shift(value, step):
    return lax.ppermute(value, "x", [(i, (i + step) % 4) for i in range(4)])


def swap_core(value):
    return lax.ppermute(value, "c", [(0, 1), (1, 0)])


def exchange(value):
    return lax.all_to_all(value, ("z", "y"), split_axis=0, concat_axis=0, tiled=True)


def own_first(start):
    return jnp.minimum(3 * start, 7)


def sum_dp(partial_value, squares):
    core = lax.axis_index("c")
    body = partial_value.reshape(64, 16, 256)
    tail = jnp.pad(pieces(squares)[:, None, :], ((0, 0), (0, 15), (0, 125)))
    whole = jnp.concatenate([body, tail], axis=2).astype(BF)
    got = swap_core(lax.dynamic_slice_in_dim(whole, 32 * (1 - core), 32, 0))
    kept = lax.dynamic_slice_in_dim(whole, 32 * core, 32, 0)
    both = kept.astype(F32) + got.astype(F32)
    tail = jnp.pad(
        pieces(both[:, 0, 256] + both[:, 0, 257] + both[:, 0, 258])[:, None, :],
        ((0, 0), (0, 15), (0, 125)),
    )
    whole = jnp.concatenate([both[:, :, :256], tail], axis=2).astype(BF)
    total = jnp.sum(exchange(whole).astype(F32), axis=0)
    return total[:, :256], total[0, 256] + total[0, 257] + total[0, 258]


def gather_dp(row, length):
    core = lax.axis_index("c")
    tail = jnp.pad(pieces(length)[None, :], ((0, 15), (0, 125)))
    whole = jnp.concatenate([row, tail], axis=1).astype(BF)
    mine = exchange(jnp.broadcast_to(whole[None], (32, 16, 384)))
    other = swap_core(mine)
    both = jnp.where(
        core == 0,
        jnp.concatenate([mine, other], axis=0),
        jnp.concatenate([other, mine], axis=0),
    )
    tail = both[:, 0, 256:259].astype(F32)
    return both[:, :, :256].reshape(64, 4096), tail[:, 0] + tail[:, 1] + tail[:, 2]


def pack(chunk, squares):
    tail = jnp.pad(pieces(squares), ((0, 0), (0, 125)))
    return jnp.concatenate([chunk.astype(BF), tail.astype(BF)[None]], axis=0)


def unpack(chunk):
    tail = chunk[3, :, :3].astype(F32)
    return chunk[:3], tail[:, 0] + tail[:, 1] + tail[:, 2]


def to_model(right, coeffs):
    value = jnp.einsum(
        "rtkb,rntk->ntb", right, coeffs.reshape(10, 64, 4, 32), preferred_element_type=F32
    )
    return value.reshape(64, 4096)


def model_coeffs(right, model):
    value = jnp.einsum(
        "rtkb,ntb->rntk", right, model.reshape(64, 4, 1024), preferred_element_type=F32
    )
    value = value.reshape(10, 64, 128).astype(BF)
    return jnp.concatenate(
        [value[jnp.array(ORDER)], jnp.zeros((2, 64, 128), BF)], axis=0
    )


def on_device(left, right, observations):
    here = lax.axis_index("x")
    row_here = 32 * lax.axis_index("c") + 4 * lax.axis_index("z") + lax.axis_index("y")
    left = left.reshape(10, 128, 1024)
    right = right.reshape(10, 4, 32, 1024)
    observations = observations.reshape(10, 64, 1024)
    owned = []
    for step in range(4):
        block = lax.dynamic_slice_in_dim(left, own_first((here + step) % 4), 3, 0)
        owned.append(block if step == 0 else shift(block, step))
    owned = jnp.concatenate(owned, axis=1)[::-1]

    start = jnp.einsum("rkb,rnb->rnk", left, observations, preferred_element_type=F32)
    values = observations.astype(F32)
    squares = jnp.sum(values * values, axis=(0, 2))
    partial_model = to_model(right, start.astype(BF))
    total, squares = sum_dp(partial_model, squares)
    length = jnp.sqrt(squares + EPSILON)
    raw = total / length

    field = lax.dynamic_slice_in_dim(values, own_first(here), 3, 0)[::-1]
    valid = (here < 3) | (jnp.arange(3) == 0)
    field = jnp.where(valid[:, None, None], field, 0.0)

    models, model_lens, data_lens = [], [], []
    for sweep in range(ITERS + 1):
        gathered, data_len = gather_dp(raw, length)
        models.append(gathered)
        data_lens.append(data_len)
        wide = gathered.astype(F32)
        squares = jnp.sum(wide * wide, axis=1)
        if sweep == ITERS:
            for step in (1, 2, 3):
                squares_there = shift(jnp.sum(wide * wide, axis=1), step)
                squares = squares + squares_there
            model_lens.append(jnp.sqrt(squares + EPSILON))
            break
        slots = model_coeffs(right, gathered)
        parts = []
        for step in range(4):
            chunk = lax.dynamic_slice_in_dim(slots, 3 * ((here + step) % 4), 3, 0)
            chunk = pack(chunk, squares)
            parts.append(unpack(chunk if step == 0 else shift(chunk, step)))
        coeffs = jnp.concatenate([part[0] for part in parts], axis=2)
        model_len = jnp.sqrt(sum(part[1] for part in parts) + EPSILON)
        model_lens.append(model_len)
        product = jnp.einsum("snk,skb->snb", coeffs, owned, preferred_element_type=F32)
        field = product / model_len[:, None] - (model_len / data_len)[:, None] * field
        squares = jnp.sum(field * field, axis=(0, 2))
        back = jnp.einsum(
            "skb,snb->snk", owned, field.astype(BF), preferred_element_type=F32
        )
        slots = jnp.zeros((12, 64, 128), BF)
        total_squares = 0.0
        for step in range(4):
            chunk = pack(back[:, :, 128 * step : 128 * (step + 1)], squares)
            chunk = chunk if step == 0 else shift(chunk, -step)
            part, share = unpack(chunk)
            slots = lax.dynamic_update_slice_in_dim(slots, part, 3 * ((here + step) % 4), 0)
            total_squares = total_squares + share
        coeffs = jnp.stack([slots[ORDER.index(pair)] for pair in range(10)])
        total, squares = sum_dp(to_model(right, coeffs), total_squares)
        length = jnp.sqrt(squares + EPSILON)
        previous = raw / model_len[row_here]
        raw = total / length - length * previous

    shape = lambda value: value.reshape(64, 4, 1024).transpose(1, 0, 2)
    solution = 0.0
    direction = shape(models[0].astype(F32) / model_lens[0][:, None])
    residual_estimate = data_lens[0]
    diagonal_bar = model_lens[0]
    for sweep in range(ITERS):
        data_len, model_len = data_lens[sweep + 1], model_lens[sweep + 1]
        model = shape(models[sweep + 1].astype(F32) / model_len[:, None])
        rotation = jnp.sqrt(diagonal_bar * diagonal_bar + data_len * data_len)
        cosine_term = diagonal_bar / rotation
        sine_term = data_len / rotation
        coupling = sine_term * model_len
        diagonal_bar = -cosine_term * model_len
        step_size = cosine_term * residual_estimate
        residual_estimate = sine_term * residual_estimate
        solution = solution + (step_size / rotation)[:, None] * direction
        direction = model - (coupling / rotation)[:, None] * direction
    return solution, direction, residual_estimate


def solution(mesh):
    fine = Mesh(mesh.devices.reshape(8, 4, 2, 4), ("z", "y", "c", "x"))
    rows = ("z", "y", "c")
    return jax.shard_map(
        on_device,
        mesh=fine,
        in_specs=(
            P(rows, None, "x", None, None),
            P(rows, None, "x", None, None),
            P(rows, None, None, None),
        ),
        out_specs=(P("x", None, None), P("x", None, None), P()),
        check_vma=False,
    )
```

```python
import functools

import jax
import jax.numpy as jnp
from jax import lax
from jax.experimental import pallas as pl
from jax.experimental.pallas import tpu as pltpu
from jax.sharding import Mesh
from jax.sharding import PartitionSpec as P

ITERS = 2
EPSILON = 1e-06
ORDER = (2, 1, 0, 5, 4, 3, 8, 7, 6, 9)
BF = jnp.bfloat16
F32 = jnp.float32
VMEM_LIMIT = 40 * 1024 * 1024


def call(kernel, outs, scratch=(), name=None):
    def run(places, *operands):
        return pl.pallas_call(
            kernel,
            out_shape=[jax.ShapeDtypeStruct(shape, dtype) for shape, dtype in outs],
            in_specs=[pl.BlockSpec(memory_space=pltpu.SMEM)]
            + [pl.BlockSpec(memory_space=pltpu.VMEM)] * len(operands),
            out_specs=[pl.BlockSpec(memory_space=pltpu.VMEM)] * len(outs),
            scratch_shapes=[pltpu.VMEM(shape, dtype) for shape, dtype in scratch],
            compiler_params=pltpu.CompilerParams(vmem_limit_bytes=VMEM_LIMIT),
            name=name,
        )(places, *operands)

    return run


def dot(first, second):
    return jnp.dot(first, second, preferred_element_type=F32)


def dot_nt(first, second):
    return lax.dot_general(
        first, second, (((1,), (1,)), ((), ())), preferred_element_type=F32
    )


def split(value):
    first = value.astype(BF).astype(F32)
    rest = value - first
    second = rest.astype(BF).astype(F32)
    return first, second, (rest - second).astype(BF).astype(F32)


def lane_sum(value):
    return jnp.sum(value, axis=-1, keepdims=True)


def pieces_in_lanes(column):
    first, second, third = split(column)
    lane = lax.broadcasted_iota(jnp.int32, (64, 128), 1)
    return jnp.where(
        lane == 0, first, jnp.where(lane == 1, second, jnp.where(lane == 2, third, 0.0))
    )


def pieces_in_rows(row):
    first, second, third = split(row)
    at = lax.broadcasted_iota(jnp.int32, (8, 128), 0)
    return jnp.where(
        at == 0, first, jnp.where(at == 1, second, jnp.where(at == 2, third, 0.0))
    )


def diagonal():
    return lax.broadcasted_iota(jnp.int32, (64, 128), 0) == lax.broadcasted_iota(
        jnp.int32, (64, 128), 1
    )


def to_row(column):
    return jnp.sum(jnp.where(diagonal(), column, 0.0), axis=0, keepdims=True)


def to_column(row):
    return lane_sum(jnp.where(diagonal(), row, 0.0))


def write_partial(places, coeffs, right, squares, keep, send, field):
    for t in range(4):
        factors = jnp.concatenate([right[pair, t] for pair in ORDER], axis=0)
        value = dot(coeffs(t), factors)
        for i in range(8):
            field[i % 4, pl.ds(2 * t + i // 4, 64, stride=8), :] = value[
                :, 128 * i : 128 * i + 128
            ]
    core = places[1]
    kept = pl.ds(pl.multiple_of(256 * core, 256), 256)
    sent = pl.ds(pl.multiple_of(256 * (1 - core), 256), 256)
    for i in range(4):
        keep[:, 128 * i : 128 * i + 128] = field[i, kept, :]
        send[:, 128 * i : 128 * i + 128] = field[i, sent, :].astype(BF)
    tail = jnp.concatenate([pieces_in_rows(to_row(squares))] * 32, axis=0)
    keep[:, 512:640] = tail
    send[:, 512:640] = tail.astype(BF)


def start_kernel(places, left, right, observations, keep, send, field, slots):
    total = jnp.zeros((64, 128), F32)
    for j, pair in enumerate(ORDER):
        values = observations[pair]
        wide = values.astype(F32)
        wide = wide * wide
        total = total + sum(wide[:, 128 * i : 128 * i + 128] for i in range(8))
        slots[j] = dot_nt(values, left[pair]).astype(BF)
    coeffs = lambda t: jnp.concatenate(
        [slots[j][:, 32 * t : 32 * t + 32] for j in range(10)], axis=1
    )
    write_partial(places, coeffs, right, lane_sum(total), keep, send, field)


def back_kernel(places, right, own, one, two, three, keep, send, field, slots):
    here = places[0]
    squares = jnp.zeros((64, 1), F32)
    for step, chunk in enumerate((own, one, two, three)):
        at = 3 * lax.rem(here + step, 4)
        for i in range(3):
            slots[at + i] = chunk[i]
        squares = squares + lane_sum(chunk[3].astype(F32))
    coeffs = lambda t: jnp.concatenate(
        [slots[j][:, 32 * t : 32 * t + 32] for j in range(10)], axis=1
    )
    write_partial(places, coeffs, right, squares, keep, send, field)


def core_kernel(places, keep, got, out):
    both = keep[...] + got[...].astype(F32)
    out[:, 0:512] = both[:, 0:512].astype(BF)
    tail = pieces_in_rows(jnp.sum(both[0:8, 512:640], axis=0, keepdims=True))
    out[:, 512:640] = jnp.concatenate([tail] * 32, axis=0).astype(BF)


def shard_kernel(first, places, got, *refs):
    previous, model_len = (None, None) if first else refs[:2]
    raw, data_len, send = refs[0 if first else 2 :][:3]
    total = jnp.sum(got[...].astype(F32).reshape(32, 8, 640), axis=0)
    squares = jnp.sum(total[:, 512:640], axis=0, keepdims=True)
    data_len[...] = jnp.broadcast_to(
        to_column(jnp.sqrt(squares + EPSILON)), (64, 128)
    )
    row = places[2]
    length = data_len[pl.ds(row, 1), 0:1]
    value = total[:, 0:512] / length
    if not first:
        value = value - (length / model_len[pl.ds(row, 1), 0:1]) * previous[...]
    raw[...] = value
    send[...] = jnp.concatenate([value] * 32, axis=0).astype(BF)


def read_model(places, mine, other, model, field):
    core = places[1]
    here = pl.ds(pl.multiple_of(256 * core, 256), 256)
    there = pl.ds(pl.multiple_of(256 * (1 - core), 256), 256)
    for i in range(4):
        field[i, here, :] = mine[:, 128 * i : 128 * i + 128].astype(F32)
        field[i, there, :] = other[:, 128 * i : 128 * i + 128].astype(F32)
    total = jnp.zeros((64, 128), F32)
    for at in range(32):
        value = field[at % 4, pl.ds(at // 4, 64, stride=8), :]
        model[:, 128 * at : 128 * at + 128] = value.astype(BF)
        total = total + value * value
    return lane_sum(total)


def forward_kernel(places, mine, other, right, model, own, one, two, three, field, slots):
    squares = read_model(places, mine, other, model, field)
    for t in range(4):
        factors = jnp.concatenate([right[pair, t] for pair in ORDER], axis=0)
        value = dot_nt(model[:, 1024 * t : 1024 * t + 1024], factors).astype(BF)
        for j in range(10):
            slots[j, :, 32 * t : 32 * t + 32] = value[:, 32 * j : 32 * j + 32]
    for j in (10, 11):
        slots[j] = jnp.zeros((64, 128), BF)
    tail = pieces_in_lanes(squares).astype(BF)
    here = places[0]
    for step, chunk in enumerate((own, one, two, three)):
        at = 3 * lax.rem(here + step, 4)
        for i in range(3):
            chunk[i] = slots[at + i]
        chunk[3] = tail


def data_kernel(last, places, *refs):
    coeffs, left, (field, data_len), refs = refs[:4], refs[4:8], refs[8:10], refs[10:]
    model_len, outs = refs[0], refs[1:5]
    squares = sum(lane_sum(chunk[3].astype(F32)) for chunk in coeffs)
    length = jnp.sqrt(squares + EPSILON)
    model_len[...] = jnp.broadcast_to(length, (64, 128))
    inverse = 1.0 / length
    ratio = length / data_len[:, 0:1]
    total = jnp.zeros((64, 128), F32)
    for i in range(3):
        factors = jnp.concatenate([block[2 - i] for block in left], axis=0)
        value = dot(jnp.concatenate([chunk[i] for chunk in coeffs], axis=1), factors)
        value = value * inverse - ratio * field[i]
        if not last:
            refs[5][i] = value
        back = dot_nt(value.astype(BF), factors).astype(BF)
        for step in range(4):
            outs[step][i] = back[:, 128 * step : 128 * step + 128]
        value = value * value
        total = total + sum(value[:, 128 * k : 128 * k + 128] for k in range(8))
    tail = pieces_in_lanes(lane_sum(total)).astype(BF)
    for step in range(4):
        outs[step][3] = tail


def last_model_kernel(places, mine, other, model, squares, field):
    squares[...] = jnp.broadcast_to(
        read_model(places, mine, other, model, field), (64, 128)
    )


def scalars(data_lens, model_lens):
    diagonal_bar, residual = model_lens[0], data_lens[0]
    out = []
    for sweep in range(ITERS):
        data_len = data_lens[sweep + 1]
        rotation = jnp.sqrt(diagonal_bar * diagonal_bar + data_len * data_len)
        cosine_term = diagonal_bar / rotation
        sine_term = data_len / rotation
        into_solution = (cosine_term * residual) / rotation
        residual = sine_term * residual
        into_direction = None
        if sweep + 1 < len(model_lens):
            into_direction = (sine_term * model_lens[sweep + 1]) / rotation
            diagonal_bar = -cosine_term * model_lens[sweep + 1]
        out.append((into_solution, into_direction))
    return out, residual


def solution_kernel(places, *refs):
    data_lens, model_lens, (first, second) = refs[:3], refs[3:5], refs[5:7]
    solved, residual_estimate, last_direction = refs[7:]
    model_lens = [ref[:, 0:1] for ref in model_lens]
    steps, residual = scalars([ref[:, 0:1] for ref in data_lens], model_lens)
    residual_estimate[...] = jnp.broadcast_to(residual, (64, 128))
    for t in range(4):
        part = slice(1024 * t, 1024 * t + 1024)
        direction = first[:, part].astype(F32) / model_lens[0]
        value = steps[0][0] * direction
        direction = second[:, part].astype(F32) / model_lens[1] - steps[0][1] * direction
        solved[t] = value + steps[1][0] * direction
        last_direction[t] = direction


def direction_kernel(places, *refs):
    data_lens, model_lens, squares, (third, last_direction, out) = (
        refs[:3],
        refs[3:5],
        refs[5:9],
        refs[9:],
    )
    length = jnp.sqrt(sum(ref[:, 0:1] for ref in squares) + EPSILON)
    model_lens = [ref[:, 0:1] for ref in model_lens] + [length]
    steps, residual = scalars([ref[:, 0:1] for ref in data_lens], model_lens)
    for t in range(4):
        model = third[:, 1024 * t : 1024 * t + 1024].astype(F32) / length
        out[t] = model - steps[1][1] * last_direction[t]


def shift(value, step):
    return lax.ppermute(value, "x", [(i, (i + step) % 4) for i in range(4)])


def swap_core(value):
    return lax.ppermute(value, "c", [(0, 1), (1, 0)])


def exchange(value):
    width = value.shape[1]
    value = lax.all_to_all(
        value.reshape(32, 8, width), ("z", "y"), split_axis=0, concat_axis=0, tiled=True
    )
    return value.reshape(256, width)


PARTIAL = [((256, 640), F32), ((256, 640), BF)]
PARTIAL_SCRATCH = [((4, 512, 128), F32), ((12, 64, 128), BF)]
CHUNKS = [((4, 64, 128), BF)] * 4
COLUMN = ((64, 128), F32)
MODEL = ((64, 4096), BF)


def on_device(left, right, observations):
    here = lax.axis_index("x")
    core = lax.axis_index("c")
    row = 32 * core + 4 * lax.axis_index("z") + lax.axis_index("y")
    places = jnp.stack([here, core, row]).astype(jnp.int32)
    left = left.reshape(10, 128, 1024)
    right = right.reshape(10, 4, 32, 1024)
    observations = observations.reshape(10, 64, 1024)
    own_first = lambda device: jnp.minimum(3 * device, 7)
    owned = []
    for step in range(4):
        block = lax.dynamic_slice_in_dim(left, own_first((here + step) % 4), 3, 0)
        owned.append(block if step == 0 else shift(block, step))
    field = lax.dynamic_slice_in_dim(observations, own_first(here), 3, 0)[::-1]
    valid = (here < 3) | (jnp.arange(3) == 0)
    field = jnp.where(valid[:, None, None], field.astype(F32), 0.0)

    def sum_dp(keep, send, first, *extra):
        whole = call(core_kernel, [((256, 640), BF)], name="core_sum")(
            places, keep, swap_core(send)
        )[0]
        raw, data_len, send = call(
            functools.partial(shard_kernel, first),
            [((8, 512), F32), COLUMN, ((256, 512), BF)],
            name="shard",
        )(places, exchange(whole), *extra)
        mine = exchange(send)
        return raw, data_len, mine, swap_core(mine)

    keep, send = call(start_kernel, PARTIAL, PARTIAL_SCRATCH, name="start")(
        places, left, right, observations
    )
    raw, data_len, mine, other = sum_dp(keep, send, True)
    models, model_lens, data_lens = [], [], [data_len]
    for sweep in range(ITERS):
        model, *chunks = call(
            forward_kernel,
            [MODEL] + CHUNKS,
            [((4, 512, 128), F32), ((12, 64, 128), BF)],
            name="forward",
        )(places, mine, other, right)
        models.append(model)
        chunks = [chunks[0]] + [shift(chunks[step], step) for step in (1, 2, 3)]
        last = sweep == ITERS - 1
        outs = call(
            functools.partial(data_kernel, last),
            [COLUMN] + CHUNKS + ([] if last else [((3, 64, 1024), F32)]),
            name="data",
        )(places, *chunks, *owned, field, data_lens[-1])
        model_lens.append(outs[0])
        field = None if last else outs[5]
        chunks = [outs[1]] + [shift(outs[1 + step], -step) for step in (1, 2, 3)]
        keep, send = call(back_kernel, PARTIAL, PARTIAL_SCRATCH, name="back")(
            places, right, *chunks
        )
        raw, data_len, mine, other = sum_dp(keep, send, False, raw, model_lens[-1])
        data_lens.append(data_len)

    model, squares = call(
        last_model_kernel, [MODEL, COLUMN], [((4, 512, 128), F32)], name="last_model"
    )(places, mine, other)
    squares = [squares] + [shift(squares, step) for step in (1, 2, 3)]
    solved, residual, last_direction = call(
        solution_kernel,
        [((4, 64, 1024), F32), COLUMN, ((4, 64, 1024), F32)],
        name="solve",
    )(places, *data_lens, *model_lens, *models)
    direction = call(direction_kernel, [((4, 64, 1024), F32)], name="direct")(
        places, *data_lens, *model_lens, *squares, model, last_direction
    )[0]
    return solved, direction, residual[:, 0]


def solution(mesh):
    fine = Mesh(mesh.devices.reshape(8, 4, 2, 4), ("z", "y", "c", "x"))
    rows = ("z", "y", "c")
    return jax.shard_map(
        on_device,
        mesh=fine,
        in_specs=(
            P(rows, None, "x", None, None),
            P(rows, None, "x", None, None),
            P(rows, None, None, None),
        ),
        out_specs=(P("x", None, None), P("x", None, None), P()),
        check_vma=False,
    )
```

```python
import functools

import jax
import jax.numpy as jnp
from jax import lax
from jax.experimental import pallas as pl
from jax.experimental.pallas import tpu as pltpu
from jax.sharding import Mesh
from jax.sharding import PartitionSpec as P

ITERS = 2
EPSILON = 1e-06
BF = jnp.bfloat16
F32 = jnp.float32
VMEM_LIMIT = 40 * 1024 * 1024
START_LIMIT = 60 * 1024 * 1024


def call(kernel, outs, scratch=(), name=None, limit=VMEM_LIMIT, anywhere=False, after=()):
    space = pl.ANY if anywhere else pltpu.VMEM
    given = kernel

    def run(places, *operands):
        count = 1 + len(operands)

        def kernel(*refs):
            given(*refs[:count], *refs[count + len(after) :])

        return pl.pallas_call(
            kernel,
            out_shape=[jax.ShapeDtypeStruct(out[0], out[1]) for out in outs],
            in_specs=[pl.BlockSpec(memory_space=pltpu.SMEM)]
            + [pl.BlockSpec(memory_space=space)] * len(operands)
            + [pl.BlockSpec(memory_space=pl.ANY)] * len(after),
            out_specs=[
                pl.BlockSpec(memory_space=pl.ANY if len(out) > 2 else pltpu.VMEM)
                for out in outs
            ],
            scratch_shapes=[
                pltpu.VMEM(*entry) if isinstance(entry, tuple) else entry
                for entry in scratch
            ],
            compiler_params=pltpu.CompilerParams(vmem_limit_bytes=limit),
            name=name,
        )(places, *operands, *after)

    return run


def dot(first, second):
    return jnp.dot(first, second, preferred_element_type=F32)


def dot_nt(first, second):
    return lax.dot_general(
        first, second, (((1,), (1,)), ((), ())), preferred_element_type=F32
    )


def split(value):
    first = value.astype(BF).astype(F32)
    rest = value - first
    second = rest.astype(BF).astype(F32)
    return first, second, (rest - second).astype(BF).astype(F32)


def lane_sum(value):
    return jnp.sum(value, axis=-1, keepdims=True)


def pieces_in_lanes(column):
    first, second, third = split(column)
    lane = lax.broadcasted_iota(jnp.int32, (64, 128), 1)
    return jnp.where(
        lane == 0, first, jnp.where(lane == 1, second, jnp.where(lane == 2, third, 0.0))
    )


def pieces_in_rows(row):
    first, second, third = split(row)
    at = lax.broadcasted_iota(jnp.int32, (8, 128), 0)
    return jnp.where(
        at == 0, first, jnp.where(at == 1, second, jnp.where(at == 2, third, 0.0))
    )


def diagonal():
    return lax.broadcasted_iota(jnp.int32, (64, 128), 0) == lax.broadcasted_iota(
        jnp.int32, (64, 128), 1
    )


def to_row(column):
    return jnp.sum(jnp.where(diagonal(), column, 0.0), axis=0, keepdims=True)


def to_column(row):
    return lane_sum(jnp.where(diagonal(), row, 0.0))


def write_partial(places, coeffs, right, squares, keep, send, field):
    for t in range(4):
        factors = jnp.concatenate([right[pair, t] for pair in range(10)], axis=0)
        value = dot(coeffs(t), factors)
        for i in range(8):
            field[i % 4, pl.ds(2 * t + i // 4, 64, stride=8), :] = value[
                :, 128 * i : 128 * i + 128
            ]
    core = places[1]
    kept = pl.ds(pl.multiple_of(256 * core, 256), 256)
    sent = pl.ds(pl.multiple_of(256 * (1 - core), 256), 256)
    for i in range(4):
        keep[:, 128 * i : 128 * i + 128] = field[i, kept, :]
        send[:, 128 * i : 128 * i + 128] = field[i, sent, :].astype(BF)
    tail = jnp.concatenate([pieces_in_rows(to_row(squares))] * 32, axis=0)
    keep[:, 512:640] = tail
    send[:, 512:640] = tail.astype(BF)


def in_slots(slots):
    return lambda t: jnp.concatenate(
        [slots[j][:, 32 * t : 32 * t + 32] for j in range(10)], axis=1
    )


def start_kernel(
    places, left, right, observations, keep, send, one, two, three, own, own_field,
    field, slots, left_here, right_here, values_here, in_sems, out_sems,
):
    here = places[0]
    loads = []
    for pair in range(10):
        loads.append(
            (
                pltpu.make_async_copy(
                    observations.at[pair], values_here.at[pair], in_sems.at[2 * pair]
                ),
                pltpu.make_async_copy(
                    left.at[pair], left_here.at[pair], in_sems.at[2 * pair + 1]
                ),
            )
        )
    right_loads = [
        pltpu.make_async_copy(right.at[:, t], right_here.at[:, t], in_sems.at[20 + t])
        for t in range(4)
    ]
    for first, second in loads:
        first.start()
        second.start()
    for load in right_loads:
        load.start()
    total = jnp.zeros((64, 128), F32)
    for pair, (first, second) in enumerate(loads):
        first.wait()
        values = values_here[pair]
        wide = values.astype(F32)
        wide = wide * wide
        total = total + sum(wide[:, 128 * i : 128 * i + 128] for i in range(8))
        second.wait()
        slots[pair] = dot_nt(values, left_here[pair]).astype(BF)
    stores = []
    for step, out in enumerate((own, one, two, three)):
        peer = lax.rem(here + step, 4)
        half = pl.ds(pl.multiple_of(512 * lax.rem(peer, 2), 512), 512)
        at = 5 * step
        for unit in range(4):
            source = left_here.at[2 * peer + unit // 2, :, pl.ds(512 * (unit % 2), 512)]
            stores.append(
                pltpu.make_async_copy(source, out.at[unit], out_sems.at[at + unit])
            )
        source = left_here.at[8 + peer // 2, :, half]
        stores.append(pltpu.make_async_copy(source, out.at[4], out_sems.at[at + 4]))
    half = pl.ds(pl.multiple_of(512 * lax.rem(here, 2), 512), 512)
    for unit in range(4):
        source = values_here.at[2 * here + unit // 2, :, pl.ds(512 * (unit % 2), 512)]
        stores.append(
            pltpu.make_async_copy(source, own_field.at[unit], out_sems.at[20 + unit])
        )
    source = values_here.at[8 + here // 2, :, half]
    stores.append(pltpu.make_async_copy(source, own_field.at[4], out_sems.at[24]))
    for store in stores:
        store.start()
    for load in right_loads:
        load.wait()
    write_partial(places, in_slots(slots), right_here, lane_sum(total), keep, send, field)
    for store in stores:
        store.wait()


def back_kernel(places, right, own, one, two, three, keep, send, field, slots, shared):
    here = places[0]
    squares = jnp.zeros((64, 1), F32)
    for step, chunk in enumerate((own, one, two, three)):
        peer = lax.rem(here + step, 4)
        slots[2 * peer] = chunk[0]
        slots[2 * peer + 1] = chunk[1]
        shared[peer] = chunk[2].astype(F32)
        squares = squares + lane_sum(chunk[3].astype(F32))
    slots[8] = (shared[0] + shared[1]).astype(BF)
    slots[9] = (shared[2] + shared[3]).astype(BF)
    write_partial(places, in_slots(slots), right, squares, keep, send, field)


def core_kernel(places, keep, got, out):
    both = keep[...] + got[...].astype(F32)
    out[:, 0:512] = both[:, 0:512].astype(BF)
    tail = pieces_in_rows(jnp.sum(both[0:8, 512:640], axis=0, keepdims=True))
    out[:, 512:640] = jnp.concatenate([tail] * 32, axis=0).astype(BF)


def shard_kernel(first, places, got, *refs):
    previous, model_len = (None, None) if first else refs[:2]
    raw, data_len, send = refs[0 if first else 2 :][:3]
    total = jnp.sum(got[...].astype(F32).reshape(32, 8, 640), axis=0)
    squares = jnp.sum(total[:, 512:640], axis=0, keepdims=True)
    data_len[...] = jnp.broadcast_to(
        to_column(jnp.sqrt(squares + EPSILON)), (64, 128)
    )
    row = places[2]
    length = data_len[pl.ds(row, 1), 0:1]
    value = total[:, 0:512] / length
    if not first:
        value = value - (length / model_len[pl.ds(row, 1), 0:1]) * previous[...]
    raw[...] = value
    send[...] = jnp.concatenate([value] * 32, axis=0).astype(BF)


def read_model(places, mine, other, model, field):
    core = places[1]
    here = pl.ds(pl.multiple_of(256 * core, 256), 256)
    there = pl.ds(pl.multiple_of(256 * (1 - core), 256), 256)
    for i in range(4):
        field[i, here, :] = mine[:, 128 * i : 128 * i + 128].astype(F32)
        field[i, there, :] = other[:, 128 * i : 128 * i + 128].astype(F32)
    total = jnp.zeros((64, 128), F32)
    for at in range(32):
        value = field[at % 4, pl.ds(at // 4, 64, stride=8), :]
        model[:, 128 * at : 128 * at + 128] = value.astype(BF)
        total = total + value * value
    return lane_sum(total)


def forward_kernel(places, mine, other, right, model, own, one, two, three, field, slots):
    squares = read_model(places, mine, other, model, field)
    for t in range(4):
        factors = jnp.concatenate([right[pair, t] for pair in range(10)], axis=0)
        value = dot_nt(model[:, 1024 * t : 1024 * t + 1024], factors).astype(BF)
        for j in range(10):
            slots[j, :, 32 * t : 32 * t + 32] = value[:, 32 * j : 32 * j + 32]
    tail = pieces_in_lanes(squares).astype(BF)
    here = places[0]
    for step, chunk in enumerate((own, one, two, three)):
        peer = lax.rem(here + step, 4)
        chunk[0] = slots[2 * peer]
        chunk[1] = slots[2 * peer + 1]
        chunk[2] = slots[8 + peer // 2]
        chunk[3] = tail


def data_kernel(last, places, *refs):
    coeffs, left, (field, data_len), refs = refs[:4], refs[4:8], refs[8:10], refs[10:]
    model_len, outs = refs[0], refs[1:5]
    squares = sum(lane_sum(chunk[3].astype(F32)) for chunk in coeffs)
    length = jnp.sqrt(squares + EPSILON)
    model_len[...] = jnp.broadcast_to(length, (64, 128))
    inverse = 1.0 / length
    ratio = length / data_len[:, 0:1]
    total = jnp.zeros((64, 128), F32)
    for i in range(3):
        given = jnp.concatenate([chunk[i] for chunk in coeffs], axis=1)
        back = None
        for unit in range(2 * i, min(2 * i + 2, 5)):
            factors = jnp.concatenate([block[unit] for block in left], axis=0)
            value = dot(given, factors) * inverse - ratio * field[unit].astype(F32)
            if not last:
                refs[5][unit] = value
            term = dot_nt(value.astype(BF), factors)
            back = term if back is None else back + term
            value = value * value
            total = total + sum(value[:, 128 * k : 128 * k + 128] for k in range(4))
        back = back.astype(BF)
        for step in range(4):
            outs[step][i] = back[:, 128 * step : 128 * step + 128]
    tail = pieces_in_lanes(lane_sum(total)).astype(BF)
    for step in range(4):
        outs[step][3] = tail


def last_model_kernel(places, mine, other, model, squares, field):
    squares[...] = jnp.broadcast_to(
        read_model(places, mine, other, model, field), (64, 128)
    )


def scalars(data_lens, model_lens):
    diagonal_bar, residual = model_lens[0], data_lens[0]
    out = []
    for sweep in range(ITERS):
        data_len = data_lens[sweep + 1]
        rotation = jnp.sqrt(diagonal_bar * diagonal_bar + data_len * data_len)
        cosine_term = diagonal_bar / rotation
        sine_term = data_len / rotation
        into_solution = (cosine_term * residual) / rotation
        residual = sine_term * residual
        into_direction = None
        if sweep + 1 < len(model_lens):
            into_direction = (sine_term * model_lens[sweep + 1]) / rotation
            diagonal_bar = -cosine_term * model_lens[sweep + 1]
        out.append((into_solution, into_direction))
    return out, residual


def solution_kernel(places, *refs):
    data_lens, model_lens, (first, second) = refs[:3], refs[3:5], refs[5:7]
    solved, residual_estimate, last_direction = refs[7:]
    model_lens = [ref[:, 0:1] for ref in model_lens]
    steps, residual = scalars([ref[:, 0:1] for ref in data_lens], model_lens)
    residual_estimate[...] = jnp.broadcast_to(residual, (64, 128))
    for t in range(4):
        part = slice(1024 * t, 1024 * t + 1024)
        direction = first[:, part].astype(F32) / model_lens[0]
        value = steps[0][0] * direction
        direction = second[:, part].astype(F32) / model_lens[1] - steps[0][1] * direction
        solved[t] = value + steps[1][0] * direction
        last_direction[t] = direction


def direction_kernel(places, *refs):
    data_lens, model_lens, squares, (third, last_direction, out) = (
        refs[:3],
        refs[3:5],
        refs[5:9],
        refs[9:],
    )
    length = jnp.sqrt(sum(ref[:, 0:1] for ref in squares) + EPSILON)
    model_lens = [ref[:, 0:1] for ref in model_lens] + [length]
    steps, residual = scalars([ref[:, 0:1] for ref in data_lens], model_lens)
    for t in range(4):
        model = third[:, 1024 * t : 1024 * t + 1024].astype(F32) / length
        out[t] = model - steps[1][1] * last_direction[t]


def shift(value, step):
    return lax.ppermute(value, "x", [(i, (i + step) % 4) for i in range(4)])


def swap_core(value):
    return lax.ppermute(value, "c", [(0, 1), (1, 0)])


def exchange(value):
    width = value.shape[1]
    value = lax.all_to_all(
        value.reshape(32, 8, width), ("z", "y"), split_axis=0, concat_axis=0, tiled=True
    )
    return value.reshape(256, width)


PARTIAL = [((256, 640), F32), ((256, 640), BF)]
PARTIAL_SCRATCH = [((4, 512, 128), F32), ((10, 64, 128), BF)]
CHUNKS = [((4, 64, 128), BF)] * 4
COLUMN = ((64, 128), F32)
MODEL = ((64, 4096), BF)


def on_device(left, right, observations):
    here = lax.axis_index("x")
    core = lax.axis_index("c")
    row = 32 * core + 4 * lax.axis_index("z") + lax.axis_index("y")
    places = jnp.stack([here, core, row]).astype(jnp.int32)
    left = left.reshape(10, 128, 1024)
    right = right.reshape(10, 4, 32, 1024)
    observations = observations.reshape(10, 64, 1024)

    def sum_dp(keep, send, extra, before_shard=()):
        whole = call(core_kernel, [((256, 640), BF)], name="core_sum")(
            places, keep, swap_core(send)
        )[0]
        raw, data_len, send = call(
            functools.partial(shard_kernel, not extra),
            [((8, 512), F32), COLUMN, ((256, 512), BF)],
            name="shard",
            after=before_shard,
        )(places, exchange(whole), *extra)
        mine = exchange(send)
        return raw, data_len, mine, swap_core(mine)

    keep, send, one, two, three, own, field = call(
        start_kernel,
        PARTIAL + [((5, 128, 512), BF, True)] * 4 + [((5, 64, 512), BF, True)],
        PARTIAL_SCRATCH
        + [
            ((10, 128, 1024), BF),
            ((10, 4, 32, 1024), BF),
            ((10, 64, 1024), BF),
            pltpu.SemaphoreType.DMA((24,)),
            pltpu.SemaphoreType.DMA((25,)),
        ],
        name="start",
        limit=START_LIMIT,
        anywhere=True,
    )(places, left, right, observations)
    one, two, three = shift(one, 1), shift(two, 2), shift(three, 3)
    owned = [own, one, two, three]
    raw, data_len, mine, other = sum_dp(keep, send, (), (one, three))
    models, model_lens, data_lens = [], [], [data_len]
    for sweep in range(ITERS):
        model, *chunks = call(
            forward_kernel,
            [MODEL] + CHUNKS,
            [((4, 512, 128), F32), ((10, 64, 128), BF)],
            name="forward",
            after=(two,) if sweep == 0 else (),
        )(places, mine, other, right)
        models.append(model)
        chunks = [chunks[0]] + [shift(chunks[step], step) for step in (1, 2, 3)]
        last = sweep == ITERS - 1
        outs = call(
            functools.partial(data_kernel, last),
            [COLUMN] + CHUNKS + ([] if last else [((5, 64, 512), F32)]),
            name="data",
        )(places, *chunks, *owned, field, data_lens[-1])
        model_lens.append(outs[0])
        field = None if last else outs[5]
        chunks = [outs[1]] + [shift(outs[1 + step], -step) for step in (1, 2, 3)]
        keep, send = call(
            back_kernel, PARTIAL, PARTIAL_SCRATCH + [((4, 64, 128), F32)], name="back"
        )(places, right, *chunks)
        raw, data_len, mine, other = sum_dp(keep, send, (raw, model_lens[-1]))
        data_lens.append(data_len)

    model, squares = call(
        last_model_kernel, [MODEL, COLUMN], [((4, 512, 128), F32)], name="last_model"
    )(places, mine, other)
    solve_after = (squares,)
    squares = [squares] + [shift(squares, step) for step in (1, 2, 3)]
    solved, residual, last_direction = call(
        solution_kernel,
        [((4, 64, 1024), F32), COLUMN, ((4, 64, 1024), F32)],
        name="solve",
        after=solve_after,
    )(places, *data_lens, *model_lens, *models)
    direction = call(direction_kernel, [((4, 64, 1024), F32)], name="direct")(
        places, *data_lens, *model_lens, *squares, model, last_direction
    )[0]
    return solved, direction, residual[:, 0]


def solution(mesh):
    fine = Mesh(mesh.devices.reshape(8, 4, 2, 4), ("z", "y", "c", "x"))
    rows = ("z", "y", "c")
    return jax.shard_map(
        on_device,
        mesh=fine,
        in_specs=(
            P(rows, None, "x", None, None),
            P(rows, None, "x", None, None),
            P(rows, None, None, None),
        ),
        out_specs=(P("x", None, None), P("x", None, None), P()),
        check_vma=False,
    )
```

```python
import functools

import jax
import jax.numpy as jnp
from jax import lax
from jax.experimental import pallas as pl
from jax.experimental.pallas import tpu as pltpu
from jax.sharding import Mesh
from jax.sharding import PartitionSpec as P

ITERS = 2
EPSILON = 1e-06
BF = jnp.bfloat16
F32 = jnp.float32
VMEM_LIMIT = 24 * 1024 * 1024
LOADING_LIMIT = 52 * 1024 * 1024


def call(kernel, outs, scratch=(), name=None, space=pltpu.VMEM, after=(), limit=VMEM_LIMIT):
    given = kernel

    def run(*operands):
        count = len(operands)

        def kernel(*refs):
            core = lax.axis_index("c")
            row = 32 * core + 4 * lax.axis_index("z") + lax.axis_index("y")
            places = (lax.axis_index("x"), core, row)
            given(places, *refs[:count], *refs[count + len(after) :])

        return pl.pallas_call(
            kernel,
            out_shape=[jax.ShapeDtypeStruct(out[0], out[1]) for out in outs],
            in_specs=[pl.BlockSpec(memory_space=space)] * len(operands)
            + [pl.BlockSpec(memory_space=pl.ANY)] * len(after),
            out_specs=[pl.BlockSpec(memory_space=pltpu.VMEM)] * len(outs),
            scratch_shapes=[
                pltpu.VMEM(*entry) if isinstance(entry, tuple) else entry
                for entry in scratch
            ],
            compiler_params=pltpu.CompilerParams(vmem_limit_bytes=limit),
            name=name,
        )(*operands, *after)

    return run


def dot(first, second):
    return jnp.dot(first, second, preferred_element_type=F32)


def dot_nt(first, second):
    return lax.dot_general(
        first, second, (((1,), (1,)), ((), ())), preferred_element_type=F32
    )


def split(value):
    first = value.astype(BF).astype(F32)
    rest = value - first
    second = rest.astype(BF).astype(F32)
    return first, second, (rest - second).astype(BF).astype(F32)


def lane_sum(value):
    return jnp.sum(value, axis=-1, keepdims=True)


def pieces_in_lanes(column):
    first, second, third = split(column)
    lane = lax.broadcasted_iota(jnp.int32, (64, 128), 1)
    return jnp.where(
        lane == 0, first, jnp.where(lane == 1, second, jnp.where(lane == 2, third, 0.0))
    )


def pieces_in_rows(row):
    first, second, third = split(row)
    at = lax.broadcasted_iota(jnp.int32, (8, 128), 0)
    return jnp.where(
        at == 0, first, jnp.where(at == 1, second, jnp.where(at == 2, third, 0.0))
    )


def diagonal():
    return lax.broadcasted_iota(jnp.int32, (64, 128), 0) == lax.broadcasted_iota(
        jnp.int32, (64, 128), 1
    )


def to_row(column):
    return jnp.sum(jnp.where(diagonal(), column, 0.0), axis=0, keepdims=True)


def to_column(row):
    return lane_sum(jnp.where(diagonal(), row, 0.0))


def write_partial(places, coeffs, right, squares, keep, send, field, loads=None):
    for t in range(4):
        if loads:
            loads[t].wait()
        factors = jnp.concatenate([right[pair, t] for pair in range(10)], axis=0)
        value = dot(coeffs(t), factors)
        for i in range(8):
            field[i % 4, pl.ds(2 * t + i // 4, 64, stride=8), :] = value[
                :, 128 * i : 128 * i + 128
            ]
    core = places[1]
    kept = pl.ds(pl.multiple_of(256 * core, 256), 256)
    sent = pl.ds(pl.multiple_of(256 * (1 - core), 256), 256)
    for i in range(4):
        keep[:, 128 * i : 128 * i + 128] = field[i, kept, :]
        send[:, 128 * i : 128 * i + 128] = field[i, sent, :].astype(BF)
    tail = jnp.concatenate([pieces_in_rows(to_row(squares))] * 32, axis=0)
    keep[:, 512:640] = tail
    send[:, 512:640] = tail.astype(BF)


def in_slots(slots):
    return lambda t: jnp.concatenate(
        [slots[j][:, 32 * t : 32 * t + 32] for j in range(10)], axis=1
    )


def start_kernel(
    places, left, right, observations, keep, send, field, slots, left_here, right_here,
    values_here, sems,
):
    loads = []
    for pair in range(10):
        loads.append(
            (
                pltpu.make_async_copy(
                    observations.at[pair], values_here.at[pair], sems.at[2 * pair]
                ),
                pltpu.make_async_copy(
                    left.at[pair], left_here.at[pair], sems.at[2 * pair + 1]
                ),
            )
        )
    right_loads = [
        pltpu.make_async_copy(right.at[:, t], right_here.at[:, t], sems.at[20 + t])
        for t in range(4)
    ]
    for first, second in loads:
        first.start()
        second.start()
    for load in right_loads:
        load.start()
    total = jnp.zeros((64, 128), F32)
    for pair, (first, second) in enumerate(loads):
        first.wait()
        values = values_here[pair]
        wide = values.astype(F32)
        wide = wide * wide
        total = total + sum(wide[:, 128 * i : 128 * i + 128] for i in range(8))
        second.wait()
        slots[pair] = dot_nt(values, left_here[pair]).astype(BF)
    squares = lane_sum(total)
    write_partial(
        places, in_slots(slots), right_here, squares, keep, send, field, right_loads
    )


def pack_kernel(places, left, values, own, one, two, three, own_field, sems):
    here = places[0]
    copies = []

    def copy(source, target):
        copies.append(pltpu.make_async_copy(source, target, sems.at[len(copies)]))
        copies[-1].start()

    for step, out in enumerate((own, one, two, three)):
        peer = lax.rem(here + step, 4)
        half = pl.ds(pl.multiple_of(512 * lax.rem(peer, 2), 512), 512)
        for pair in range(2):
            for part in range(2):
                source = left.at[2 * peer + pair, :, pl.ds(512 * part, 512)]
                copy(source, out.at[2 * pair + part])
        copy(left.at[8 + peer // 2, :, half], out.at[4])
    half = pl.ds(pl.multiple_of(512 * lax.rem(here, 2), 512), 512)
    for pair in range(2):
        for part in range(2):
            source = values.at[2 * here + pair, :, pl.ds(512 * part, 512)]
            copy(source, own_field.at[2 * pair + part])
    copy(values.at[8 + here // 2, :, half], own_field.at[4])
    for started in copies:
        started.wait()


def back_kernel(places, right, own, one, two, three, keep, send, field, slots, shared):
    here = places[0]
    squares = jnp.zeros((64, 1), F32)
    for step, chunk in enumerate((own, one, two, three)):
        peer = lax.rem(here + step, 4)
        slots[2 * peer] = chunk[0]
        slots[2 * peer + 1] = chunk[1]
        shared[peer] = chunk[2].astype(F32)
        squares = squares + lane_sum(chunk[3].astype(F32))
    slots[8] = (shared[0] + shared[1]).astype(BF)
    slots[9] = (shared[2] + shared[3]).astype(BF)
    write_partial(places, in_slots(slots), right, squares, keep, send, field)


def core_kernel(places, keep, got, out):
    both = keep[...] + got[...].astype(F32)
    out[:, 0:512] = both[:, 0:512].astype(BF)
    tail = pieces_in_rows(jnp.sum(both[0:8, 512:640], axis=0, keepdims=True))
    out[:, 512:640] = jnp.concatenate([tail] * 32, axis=0).astype(BF)


def shard_kernel(first, places, got, *refs):
    previous, model_len = (None, None) if first else refs[:2]
    raw, data_len, send = refs[0 if first else 2 :][:3]
    total = jnp.sum(got[...].astype(F32).reshape(32, 8, 640), axis=0)
    squares = jnp.sum(total[:, 512:640], axis=0, keepdims=True)
    data_len[...] = jnp.broadcast_to(
        to_column(jnp.sqrt(squares + EPSILON)), (64, 128)
    )
    row = places[2]
    length = data_len[pl.ds(row, 1), 0:1]
    value = total[:, 0:512] / length
    if not first:
        value = value - (length / model_len[pl.ds(row, 1), 0:1]) * previous[...]
    raw[...] = value
    send[...] = jnp.concatenate([value] * 32, axis=0).astype(BF)


def read_model(places, mine, other, model, field):
    core = places[1]
    here = pl.ds(pl.multiple_of(256 * core, 256), 256)
    there = pl.ds(pl.multiple_of(256 * (1 - core), 256), 256)
    for i in range(4):
        field[i, here, :] = mine[:, 128 * i : 128 * i + 128].astype(F32)
        field[i, there, :] = other[:, 128 * i : 128 * i + 128].astype(F32)
    total = jnp.zeros((64, 128), F32)
    for at in range(32):
        value = field[at % 4, pl.ds(at // 4, 64, stride=8), :]
        model[:, 128 * at : 128 * at + 128] = value.astype(BF)
        total = total + value * value
    return lane_sum(total)


def forward_kernel(places, mine, other, right, model, own, one, two, three, field, slots):
    squares = read_model(places, mine, other, model, field)
    for t in range(4):
        factors = jnp.concatenate([right[pair, t] for pair in range(10)], axis=0)
        value = dot_nt(model[:, 1024 * t : 1024 * t + 1024], factors).astype(BF)
        for j in range(10):
            slots[j, :, 32 * t : 32 * t + 32] = value[:, 32 * j : 32 * j + 32]
    tail = pieces_in_lanes(squares).astype(BF)
    here = places[0]
    for step, chunk in enumerate((own, one, two, three)):
        peer = lax.rem(here + step, 4)
        chunk[0] = slots[2 * peer]
        chunk[1] = slots[2 * peer + 1]
        chunk[2] = slots[8 + peer // 2]
        chunk[3] = tail


def data_kernel(last, places, *refs):
    coeffs, left, (field, data_len), refs = refs[:4], refs[4:8], refs[8:10], refs[10:]
    model_len, outs = refs[0], refs[1:5]
    squares = sum(lane_sum(chunk[3].astype(F32)) for chunk in coeffs)
    length = jnp.sqrt(squares + EPSILON)
    model_len[...] = jnp.broadcast_to(length, (64, 128))
    inverse = 1.0 / length
    ratio = length / data_len[:, 0:1]
    total = jnp.zeros((64, 128), F32)
    for i in range(3):
        given = jnp.concatenate([chunk[i] for chunk in coeffs], axis=1)
        back = None
        for unit in range(2 * i, min(2 * i + 2, 5)):
            factors = jnp.concatenate([block[unit] for block in left], axis=0)
            value = dot(given, factors) * inverse - ratio * field[unit].astype(F32)
            if not last:
                refs[5][unit] = value
            term = dot_nt(value.astype(BF), factors)
            back = term if back is None else back + term
            value = value * value
            total = total + sum(value[:, 128 * k : 128 * k + 128] for k in range(4))
        back = back.astype(BF)
        for step in range(4):
            outs[step][i] = back[:, 128 * step : 128 * step + 128]
    tail = pieces_in_lanes(lane_sum(total)).astype(BF)
    for step in range(4):
        outs[step][3] = tail


def last_model_kernel(places, mine, other, model, squares, field):
    squares[...] = jnp.broadcast_to(
        read_model(places, mine, other, model, field), (64, 128)
    )


def scalars(data_lens, model_lens):
    diagonal_bar, residual = model_lens[0], data_lens[0]
    out = []
    for sweep in range(ITERS):
        data_len = data_lens[sweep + 1]
        rotation = jnp.sqrt(diagonal_bar * diagonal_bar + data_len * data_len)
        cosine_term = diagonal_bar / rotation
        sine_term = data_len / rotation
        into_solution = (cosine_term * residual) / rotation
        residual = sine_term * residual
        into_direction = None
        if sweep + 1 < len(model_lens):
            into_direction = (sine_term * model_lens[sweep + 1]) / rotation
            diagonal_bar = -cosine_term * model_lens[sweep + 1]
        out.append((into_solution, into_direction))
    return out, residual


def solution_kernel(places, *refs):
    data_lens, model_lens, (first, second) = refs[:3], refs[3:5], refs[5:7]
    solved, residual_estimate, last_direction = refs[7:]
    model_lens = [ref[:, 0:1] for ref in model_lens]
    steps, residual = scalars([ref[:, 0:1] for ref in data_lens], model_lens)
    residual_estimate[...] = jnp.broadcast_to(residual, (64, 128))
    for t in range(4):
        part = slice(1024 * t, 1024 * t + 1024)
        direction = first[:, part].astype(F32) / model_lens[0]
        value = steps[0][0] * direction
        direction = second[:, part].astype(F32) / model_lens[1] - steps[0][1] * direction
        solved[t] = value + steps[1][0] * direction
        last_direction[t] = direction


def direction_kernel(places, *refs):
    data_lens, model_lens, squares = refs[:3], refs[3:5], refs[5:9]
    third, last_direction, out = refs[9:]
    length = jnp.sqrt(sum(ref[:, 0:1] for ref in squares) + EPSILON)
    model_lens = [ref[:, 0:1] for ref in model_lens] + [length]
    steps, residual = scalars([ref[:, 0:1] for ref in data_lens], model_lens)
    for t in range(4):
        model = third[:, 1024 * t : 1024 * t + 1024].astype(F32) / length
        out[t] = model - steps[1][1] * last_direction[t]


def shift(value, step):
    return lax.ppermute(value, "x", [(i, (i + step) % 4) for i in range(4)])


def swap_core(value):
    return lax.ppermute(value, "c", [(0, 1), (1, 0)])


def exchange(value):
    width = value.shape[1]
    value = lax.all_to_all(
        value.reshape(32, 8, width), ("z", "y"), split_axis=0, concat_axis=0, tiled=True
    )
    return value.reshape(256, width)


PARTIAL = [((256, 640), F32), ((256, 640), BF)]
PARTIAL_SCRATCH = [((4, 512, 128), F32), ((10, 64, 128), BF)]
CHUNKS = [((4, 64, 128), BF)] * 4
COLUMN = ((64, 128), F32)
MODEL = ((64, 4096), BF)


def on_device(left, right, observations):
    left = left.reshape(10, 128, 1024)
    right = right.reshape(10, 4, 32, 1024)
    observations = observations.reshape(10, 64, 1024)

    def sum_dp(keep, send, extra, before_shard=()):
        whole = call(core_kernel, [((256, 640), BF)], name="core_sum")(keep, swap_core(send))[0]
        raw, data_len, send = call(
            functools.partial(shard_kernel, not extra),
            [((8, 512), F32), COLUMN, ((256, 512), BF)],
            name="shard",
            after=before_shard,
        )(exchange(whole), *extra)
        mine = exchange(send)
        return raw, data_len, mine, swap_core(mine)

    keep, send = call(
        start_kernel,
        PARTIAL,
        PARTIAL_SCRATCH
        + [
            ((10, 128, 1024), BF),
            ((10, 4, 32, 1024), BF),
            ((10, 64, 1024), BF),
            pltpu.SemaphoreType.DMA((24,)),
        ],
        name="start",
        space=pltpu.HBM,
        limit=LOADING_LIMIT,
    )(left, right, observations)
    own, one, two, three, field = call(
        pack_kernel,
        [((5, 128, 512), BF)] * 4 + [((5, 64, 512), BF)],
        [pltpu.SemaphoreType.DMA((25,))],
        name="pack",
        space=pltpu.HBM,
        after=(send,),
        limit=LOADING_LIMIT,
    )(left, observations)
    one, two, three = shift(one, 1), shift(two, 2), shift(three, 3)
    raw, data_len, mine, other = sum_dp(keep, send, (), (one, two, three))
    models, model_lens, data_lens = [], [], [data_len]
    for sweep in range(ITERS):
        model, *chunks = call(
            forward_kernel,
            [MODEL] + CHUNKS,
            [((4, 512, 128), F32), ((10, 64, 128), BF)],
            name="forward",
        )(mine, other, right)
        models.append(model)
        chunks = [chunks[0]] + [shift(chunks[step], step) for step in (1, 2, 3)]
        last = sweep == ITERS - 1
        outs = call(
            functools.partial(data_kernel, last),
            [COLUMN] + CHUNKS + ([] if last else [((5, 64, 512), F32)]),
            name="data",
        )(*chunks, own, one, two, three, field, data_lens[-1])
        model_lens.append(outs[0])
        field = None if last else outs[5]
        chunks = [outs[1]] + [shift(outs[1 + step], -step) for step in (1, 2, 3)]
        keep, send = call(
            back_kernel, PARTIAL, PARTIAL_SCRATCH + [((4, 64, 128), F32)], name="back"
        )(right, *chunks)
        raw, data_len, mine, other = sum_dp(keep, send, (raw, model_lens[-1]))
        data_lens.append(data_len)

    model, squares = call(
        last_model_kernel, [MODEL, COLUMN], [((4, 512, 128), F32)], name="last_model"
    )(mine, other)
    solve_after = (squares,)
    squares = [squares] + [shift(squares, step) for step in (1, 2, 3)]
    solved, residual, last_direction = call(
        solution_kernel,
        [((4, 64, 1024), F32), COLUMN, ((4, 64, 1024), F32)],
        name="solve",
        after=solve_after,
    )(*data_lens, *model_lens, *models)
    direction = call(direction_kernel, [((4, 64, 1024), F32)], name="direct")(
        *data_lens, *model_lens, *squares, model, last_direction
    )[0]
    return solved, direction, residual[:, 0]


def solution(mesh):
    fine = Mesh(mesh.devices.reshape(8, 4, 2, 4), ("z", "y", "c", "x"))
    rows = ("z", "y", "c")
    return jax.shard_map(
        on_device,
        mesh=fine,
        in_specs=(
            P(rows, None, "x", None, None),
            P(rows, None, "x", None, None),
            P(rows, None, None, None),
        ),
        out_specs=(P("x", None, None), P("x", None, None), P()),
        check_vma=False,
    )
```

```python
import functools

import jax
import jax.numpy as jnp
from jax import lax
from jax.experimental import pallas as pl
from jax.experimental.pallas import tpu as pltpu
from jax.sharding import Mesh
from jax.sharding import PartitionSpec as P

ITERS = 2
EPSILON = 1e-06
BF = jnp.bfloat16
F32 = jnp.float32
VMEM_LIMIT = 20 * 1024 * 1024


def call(kernel, outs, scratch=(), name=None, after=()):
    given = kernel

    def run(*operands):
        count = len(operands)

        def kernel(*refs):
            core = lax.axis_index("c")
            row = 32 * core + 4 * lax.axis_index("z") + lax.axis_index("y")
            places = (lax.axis_index("x"), core, row)
            given(places, *refs[:count], *refs[count + len(after) :])

        return pl.pallas_call(
            kernel,
            out_shape=[jax.ShapeDtypeStruct(out[0], out[1]) for out in outs],
            in_specs=[pl.BlockSpec(memory_space=pltpu.VMEM)] * len(operands)
            + [pl.BlockSpec(memory_space=pl.ANY)] * len(after),
            out_specs=[pl.BlockSpec(memory_space=pltpu.VMEM)] * len(outs),
            scratch_shapes=[
                pltpu.VMEM(*entry) if isinstance(entry, tuple) else entry
                for entry in scratch
            ],
            compiler_params=pltpu.CompilerParams(vmem_limit_bytes=VMEM_LIMIT),
            name=name,
        )(*operands, *after)

    return run


def dot(first, second):
    return jnp.dot(first, second, preferred_element_type=F32)


def dot_nt(first, second):
    return lax.dot_general(
        first, second, (((1,), (1,)), ((), ())), preferred_element_type=F32
    )


def split(value):
    first = value.astype(BF).astype(F32)
    rest = value - first
    second = rest.astype(BF).astype(F32)
    return first, second, (rest - second).astype(BF).astype(F32)


def lane_sum(value):
    return jnp.sum(value, axis=-1, keepdims=True)


def pieces_in_lanes(column):
    first, second, third = split(column)
    lane = lax.broadcasted_iota(jnp.int32, (64, 128), 1)
    return jnp.where(
        lane == 0, first, jnp.where(lane == 1, second, jnp.where(lane == 2, third, 0.0))
    )


def pieces_in_rows(row):
    first, second, third = split(row)
    at = lax.broadcasted_iota(jnp.int32, (8, 128), 0)
    return jnp.where(
        at == 0, first, jnp.where(at == 1, second, jnp.where(at == 2, third, 0.0))
    )


def diagonal():
    return lax.broadcasted_iota(jnp.int32, (64, 128), 0) == lax.broadcasted_iota(
        jnp.int32, (64, 128), 1
    )


def to_row(column):
    return jnp.sum(jnp.where(diagonal(), column, 0.0), axis=0, keepdims=True)


def to_column(row):
    return lane_sum(jnp.where(diagonal(), row, 0.0))


def write_partial(places, coeffs, right, squares, keep, send, field):
    for t in range(4):
        factors = jnp.concatenate([right[pair, t] for pair in range(10)], axis=0)
        value = dot(coeffs(t), factors)
        for i in range(8):
            field[i % 4, pl.ds(2 * t + i // 4, 64, stride=8), :] = value[
                :, 128 * i : 128 * i + 128
            ]
    core = places[1]
    kept = pl.ds(pl.multiple_of(256 * core, 256), 256)
    sent = pl.ds(pl.multiple_of(256 * (1 - core), 256), 256)
    for i in range(4):
        keep[:, 128 * i : 128 * i + 128] = field[i, kept, :]
        send[:, 128 * i : 128 * i + 128] = field[i, sent, :].astype(BF)
    tail = jnp.concatenate([pieces_in_rows(to_row(squares))] * 32, axis=0)
    keep[:, 512:640] = tail
    send[:, 512:640] = tail.astype(BF)


def in_slots(slots):
    return lambda t: jnp.concatenate(
        [slots[j][:, 32 * t : 32 * t + 32] for j in range(10)], axis=1
    )


def start_kernel(places, left, observations, slots, squares):
    total = jnp.zeros((64, 128), F32)
    for pair in range(10):
        values = observations[pair]
        wide = values.astype(F32)
        wide = wide * wide
        total = total + sum(wide[:, 128 * i : 128 * i + 128] for i in range(8))
        slots[pair] = dot_nt(values, left[pair]).astype(BF)
    squares[...] = jnp.broadcast_to(lane_sum(total), (64, 128))


def first_back_kernel(places, right, slots, squares, keep, send, field):
    write_partial(places, in_slots(slots), right, squares[:, 0:1], keep, send, field)


def pack_kernel(steps, places, left, *outs):
    for step, out in zip(steps, outs):
        for unit in range(5):
            out[unit] = unit_of(left, lax.rem(places[0] + step, 4), unit)


def unit_of(ref, owner, unit):
    if unit < 4:
        return ref[2 * owner + unit // 2, :, 512 * (unit % 2) : 512 * (unit % 2) + 512]
    half = pl.ds(pl.multiple_of(512 * lax.rem(owner, 2), 512), 512)
    return ref[8 + owner // 2, :, half]


def back_kernel(places, right, own, one, two, three, keep, send, field, slots, shared):
    here = places[0]
    squares = jnp.zeros((64, 1), F32)
    for step, chunk in enumerate((own, one, two, three)):
        peer = lax.rem(here + step, 4)
        slots[2 * peer] = chunk[0]
        slots[2 * peer + 1] = chunk[1]
        shared[peer] = chunk[2].astype(F32)
        squares = squares + lane_sum(chunk[3].astype(F32))
    slots[8] = (shared[0] + shared[1]).astype(BF)
    slots[9] = (shared[2] + shared[3]).astype(BF)
    write_partial(places, in_slots(slots), right, squares, keep, send, field)


def core_kernel(places, keep, got, out):
    both = keep[...] + got[...].astype(F32)
    out[:, 0:512] = both[:, 0:512].astype(BF)
    tail = pieces_in_rows(jnp.sum(both[0:8, 512:640], axis=0, keepdims=True))
    out[:, 512:640] = jnp.concatenate([tail] * 32, axis=0).astype(BF)


def shard_kernel(first, places, got, *refs):
    previous, model_len = (None, None) if first else refs[:2]
    raw, data_len, send = refs[0 if first else 2 :][:3]
    total = jnp.sum(got[...].astype(F32).reshape(32, 8, 640), axis=0)
    squares = jnp.sum(total[:, 512:640], axis=0, keepdims=True)
    data_len[...] = jnp.broadcast_to(
        to_column(jnp.sqrt(squares + EPSILON)), (64, 128)
    )
    row = places[2]
    length = data_len[pl.ds(row, 1), 0:1]
    value = total[:, 0:512] / length
    if not first:
        value = value - (length / model_len[pl.ds(row, 1), 0:1]) * previous[...]
    raw[...] = value
    send[...] = jnp.concatenate([value] * 32, axis=0).astype(BF)


def read_model(places, mine, other, model, field):
    core = places[1]
    here = pl.ds(pl.multiple_of(256 * core, 256), 256)
    there = pl.ds(pl.multiple_of(256 * (1 - core), 256), 256)
    for i in range(4):
        field[i, here, :] = mine[:, 128 * i : 128 * i + 128].astype(F32)
        field[i, there, :] = other[:, 128 * i : 128 * i + 128].astype(F32)
    total = jnp.zeros((64, 128), F32)
    for at in range(32):
        value = field[at % 4, pl.ds(at // 4, 64, stride=8), :]
        model[:, 128 * at : 128 * at + 128] = value.astype(BF)
        total = total + value * value
    return lane_sum(total)


def forward_kernel(places, mine, other, right, model, own, one, two, three, field, slots):
    squares = read_model(places, mine, other, model, field)
    for t in range(4):
        factors = jnp.concatenate([right[pair, t] for pair in range(10)], axis=0)
        value = dot_nt(model[:, 1024 * t : 1024 * t + 1024], factors).astype(BF)
        for j in range(10):
            slots[j, :, 32 * t : 32 * t + 32] = value[:, 32 * j : 32 * j + 32]
    tail = pieces_in_lanes(squares).astype(BF)
    here = places[0]
    for step, chunk in enumerate((own, one, two, three)):
        peer = lax.rem(here + step, 4)
        chunk[0] = slots[2 * peer]
        chunk[1] = slots[2 * peer + 1]
        chunk[2] = slots[8 + peer // 2]
        chunk[3] = tail


def data_kernel(last, places, *refs):
    coeffs, blocks, (left, field, data_len), refs = refs[:4], refs[4:7], refs[7:10], refs[10:]
    model_len, outs = refs[0], refs[1:5]
    squares = sum(lane_sum(chunk[3].astype(F32)) for chunk in coeffs)
    length = jnp.sqrt(squares + EPSILON)
    model_len[...] = jnp.broadcast_to(length, (64, 128))
    inverse = 1.0 / length
    ratio = length / data_len[:, 0:1]
    total = jnp.zeros((64, 128), F32)
    for i in range(3):
        given = jnp.concatenate([chunk[i] for chunk in coeffs], axis=1)
        back = None
        for unit in range(2 * i, min(2 * i + 2, 5)):
            factors = [unit_of(left, places[0], unit)] + [block[unit] for block in blocks]
            factors = jnp.concatenate(factors, axis=0)
            before = field[unit] if last else unit_of(field, places[0], unit).astype(F32)
            value = dot(given, factors) * inverse - ratio * before
            if not last:
                refs[5][unit] = value
            term = dot_nt(value.astype(BF), factors)
            back = term if back is None else back + term
            value = value * value
            total = total + sum(value[:, 128 * k : 128 * k + 128] for k in range(4))
        back = back.astype(BF)
        for step in range(4):
            outs[step][i] = back[:, 128 * step : 128 * step + 128]
    tail = pieces_in_lanes(lane_sum(total)).astype(BF)
    for step in range(4):
        outs[step][3] = tail


def last_model_kernel(places, mine, other, model, squares, field):
    squares[...] = jnp.broadcast_to(
        read_model(places, mine, other, model, field), (64, 128)
    )


def scalars(data_lens, model_lens):
    diagonal_bar, residual = model_lens[0], data_lens[0]
    out = []
    for sweep in range(ITERS):
        data_len = data_lens[sweep + 1]
        rotation = jnp.sqrt(diagonal_bar * diagonal_bar + data_len * data_len)
        cosine_term = diagonal_bar / rotation
        sine_term = data_len / rotation
        into_solution = (cosine_term * residual) / rotation
        residual = sine_term * residual
        into_direction = None
        if sweep + 1 < len(model_lens):
            into_direction = (sine_term * model_lens[sweep + 1]) / rotation
            diagonal_bar = -cosine_term * model_lens[sweep + 1]
        out.append((into_solution, into_direction))
    return out, residual


def solution_kernel(places, *refs):
    data_lens, model_lens, (first, second) = refs[:3], refs[3:5], refs[5:7]
    solved, residual_estimate, last_direction = refs[7:]
    model_lens = [ref[:, 0:1] for ref in model_lens]
    steps, residual = scalars([ref[:, 0:1] for ref in data_lens], model_lens)
    residual_estimate[...] = jnp.broadcast_to(residual, (64, 128))
    for t in range(4):
        part = slice(1024 * t, 1024 * t + 1024)
        direction = first[:, part].astype(F32) / model_lens[0]
        value = steps[0][0] * direction
        direction = second[:, part].astype(F32) / model_lens[1] - steps[0][1] * direction
        solved[t] = value + steps[1][0] * direction
        last_direction[t] = direction


def direction_kernel(places, *refs):
    data_lens, model_lens, squares = refs[:3], refs[3:5], refs[5:9]
    third, last_direction, out = refs[9:]
    length = jnp.sqrt(sum(ref[:, 0:1] for ref in squares) + EPSILON)
    model_lens = [ref[:, 0:1] for ref in model_lens] + [length]
    steps, residual = scalars([ref[:, 0:1] for ref in data_lens], model_lens)
    for t in range(4):
        model = third[:, 1024 * t : 1024 * t + 1024].astype(F32) / length
        out[t] = model - steps[1][1] * last_direction[t]


def shift(value, step):
    return lax.ppermute(value, "x", [(i, (i + step) % 4) for i in range(4)])


def swap_core(value):
    return lax.ppermute(value, "c", [(0, 1), (1, 0)])


def exchange(value):
    width = value.shape[1]
    value = lax.all_to_all(
        value.reshape(32, 8, width), ("z", "y"), split_axis=0, concat_axis=0, tiled=True
    )
    return value.reshape(256, width)


PARTIAL = [((256, 640), F32), ((256, 640), BF)]
PARTIAL_SCRATCH = [((4, 512, 128), F32), ((10, 64, 128), BF)]
CHUNKS = [((4, 64, 128), BF)] * 4
COLUMN = ((64, 128), F32)
MODEL = ((64, 4096), BF)


def on_device(left, right, observations):
    left = left.reshape(10, 128, 1024)
    right = right.reshape(10, 4, 32, 1024)
    observations = observations.reshape(10, 64, 1024)

    def sum_dp(whole, extra, before_shard=()):
        raw, data_len, send = call(
            functools.partial(shard_kernel, not extra),
            [((8, 512), F32), COLUMN, ((256, 512), BF)],
            name="shard",
            after=before_shard,
        )(exchange(whole), *extra)
        mine = exchange(send)
        return raw, data_len, mine, swap_core(mine)

    slots, squares = call(
        start_kernel, [((10, 64, 128), BF), COLUMN], name="start"
    )(left, observations)
    keep, send = call(first_back_kernel, PARTIAL, PARTIAL_SCRATCH[:1], name="start_sum")(
        right, slots, squares
    )
    block = ((5, 128, 512), BF)
    one, three = call(
        functools.partial(pack_kernel, (1, 3)), [block] * 2, name="pack", after=(send,)
    )(left)
    one, three = shift(one, 1), shift(three, 3)
    two = call(
        functools.partial(pack_kernel, (2,)), [block], name="pack_two", after=(one, three)
    )(left)[0]
    blocks = [one, shift(two, 2), three]
    whole = call(core_kernel, [((256, 640), BF)], name="core_sum")(
        keep, swap_core(send)
    )[0]
    raw, data_len, mine, other = sum_dp(whole, (), ())
    models, model_lens, data_lens = [], [], [data_len]
    for sweep in range(ITERS):
        model, *chunks = call(
            forward_kernel,
            [MODEL] + CHUNKS,
            [((4, 512, 128), F32), ((10, 64, 128), BF)],
            name="forward",
            after=() if sweep == 0 else (),
        )(mine, other, right)
        models.append(model)
        chunks = [chunks[0]] + [shift(chunks[step], step) for step in (1, 2, 3)]
        last = sweep == ITERS - 1
        outs = call(
            functools.partial(data_kernel, last),
            [COLUMN] + CHUNKS + ([] if last else [((5, 64, 512), F32)]),
            name="data",
        )(*chunks, *blocks, left, observations if sweep == 0 else field, data_lens[-1])
        model_lens.append(outs[0])
        field = None if last else outs[5]
        chunks = [outs[1]] + [shift(outs[1 + step], -step) for step in (1, 2, 3)]
        keep, send = call(
            back_kernel, PARTIAL, PARTIAL_SCRATCH + [((4, 64, 128), F32)], name="back"
        )(right, *chunks)
        whole = call(core_kernel, [((256, 640), BF)], name="core_sum")(
            keep, swap_core(send)
        )[0]
        raw, data_len, mine, other = sum_dp(whole, (raw, model_lens[-1]))
        data_lens.append(data_len)

    model, squares = call(
        last_model_kernel, [MODEL, COLUMN], [((4, 512, 128), F32)], name="last_model"
    )(mine, other)
    solve_after = (squares,)
    squares = [squares] + [shift(squares, step) for step in (1, 2, 3)]
    solved, residual, last_direction = call(
        solution_kernel,
        [((4, 64, 1024), F32), COLUMN, ((4, 64, 1024), F32)],
        name="solve",
        after=solve_after,
    )(*data_lens, *model_lens, *models)
    direction = call(direction_kernel, [((4, 64, 1024), F32)], name="direct")(
        *data_lens, *model_lens, *squares, model, last_direction
    )[0]
    return solved, direction, residual[:, 0]


def solution(mesh):
    fine = Mesh(mesh.devices.reshape(8, 4, 2, 4), ("z", "y", "c", "x"))
    rows = ("z", "y", "c")
    return jax.shard_map(
        on_device,
        mesh=fine,
        in_specs=(
            P(rows, None, "x", None, None),
            P(rows, None, "x", None, None),
            P(rows, None, None, None),
        ),
        out_specs=(P("x", None, None), P("x", None, None), P()),
        check_vma=False,
    )
```

```python
import functools

import jax
import jax.numpy as jnp
from jax import lax
from jax.experimental import pallas as pl
from jax.experimental.pallas import tpu as pltpu
from jax.sharding import Mesh
from jax.sharding import PartitionSpec as P

ITERS = 2
EPSILON = 1e-06
BF = jnp.bfloat16
F32 = jnp.float32
VMEM_LIMIT = 20 * 1024 * 1024


def call(kernel, outs, scratch=(), name=None, after=(), out_space=pltpu.VMEM):
    given = kernel

    def run(*operands):
        count = len(operands)

        def kernel(*refs):
            core = lax.axis_index("c")
            row = 32 * core + 4 * lax.axis_index("z") + lax.axis_index("y")
            places = (lax.axis_index("x"), core, row)
            given(places, *refs[:count], *refs[count + len(after) :])

        return pl.pallas_call(
            kernel,
            out_shape=[jax.ShapeDtypeStruct(out[0], out[1]) for out in outs],
            in_specs=[pl.BlockSpec(memory_space=pltpu.VMEM)] * len(operands)
            + [pl.BlockSpec(memory_space=pl.ANY)] * len(after),
            out_specs=[pl.BlockSpec(memory_space=out_space)] * len(outs),
            scratch_shapes=[
                pltpu.VMEM(*entry) if isinstance(entry, tuple) else entry
                for entry in scratch
            ],
            compiler_params=pltpu.CompilerParams(vmem_limit_bytes=VMEM_LIMIT),
            name=name,
        )(*operands, *after)

    return run


def dot(first, second):
    return jnp.dot(first, second, preferred_element_type=F32)


def dot_nt(first, second):
    return lax.dot_general(
        first, second, (((1,), (1,)), ((), ())), preferred_element_type=F32
    )


def split(value):
    first = value.astype(BF).astype(F32)
    rest = value - first
    second = rest.astype(BF).astype(F32)
    return first, second, (rest - second).astype(BF).astype(F32)


def lane_sum(value):
    return jnp.sum(value, axis=-1, keepdims=True)


def pieces_in_rows(row, count=8):
    first, second, third = split(row)
    at = lax.broadcasted_iota(jnp.int32, (count, 128), 0)
    return jnp.where(
        at == 0, first, jnp.where(at == 1, second, jnp.where(at == 2, third, 0.0))
    )


def part(index):
    return pl.ds(64 * index, 64)


TAIL = pl.ds(192, 16)


def squares_of(chunks):
    total = sum(chunk[TAIL, :].astype(F32) for chunk in chunks)
    return to_column(jnp.sum(total, axis=0, keepdims=True))


def diagonal():
    return lax.broadcasted_iota(jnp.int32, (64, 128), 0) == lax.broadcasted_iota(
        jnp.int32, (64, 128), 1
    )


def to_row(column):
    return jnp.sum(jnp.where(diagonal(), column, 0.0), axis=0, keepdims=True)


def to_column(row):
    return lane_sum(jnp.where(diagonal(), row, 0.0))


def write_partial(places, coeffs, right, squares, keep, send, field):
    for t in range(4):
        factors = jnp.concatenate([right[pair, t] for pair in range(10)], axis=0)
        value = dot(coeffs(t), factors)
        for i in range(8):
            field[i % 4, pl.ds(2 * t + i // 4, 64, stride=8), :] = value[
                :, 128 * i : 128 * i + 128
            ]
    core = places[1]
    kept = pl.ds(pl.multiple_of(256 * core, 256), 256)
    sent = pl.ds(pl.multiple_of(256 * (1 - core), 256), 256)
    for i in range(4):
        keep[:, 128 * i : 128 * i + 128] = field[i, kept, :]
        send[:, 128 * i : 128 * i + 128] = field[i, sent, :].astype(BF)
    tail = jnp.concatenate([pieces_in_rows(to_row(squares))] * 32, axis=0)
    keep[:, 512:640] = tail
    send[:, 512:640] = tail.astype(BF)


def in_slots(slots):
    return lambda t: jnp.concatenate(
        [slots[j][:, 32 * t : 32 * t + 32] for j in range(10)], axis=1
    )


def start_kernel(places, left, observations, slots, squares, own_field):
    for unit in range(5):
        own_field[unit] = unit_of(observations, places[0], unit)
    total = jnp.zeros((64, 128), F32)
    for pair in range(10):
        values = observations[pair]
        wide = values.astype(F32)
        wide = wide * wide
        total = total + sum(wide[:, 128 * i : 128 * i + 128] for i in range(8))
        slots[pair] = dot_nt(values, left[pair]).astype(BF)
    squares[...] = jnp.broadcast_to(lane_sum(total), (64, 128))


def first_back_kernel(places, right, slots, squares, keep, send, field):
    write_partial(places, in_slots(slots), right, squares[:, 0:1], keep, send, field)


def pack_kernel(places, left, one, two, three):
    here = places[0]
    for unit in range(5):
        for step, out in ((1, one), (2, two), (3, three)):
            out[unit] = unit_of(left, lax.rem(here + step, 4), unit)


def hold(value, kept=(), after=()):
    return pl.pallas_call(
        lambda *refs: None,
        out_shape=jax.ShapeDtypeStruct(value.shape, value.dtype),
        in_specs=[pl.BlockSpec(memory_space=pl.ANY)]
        + [pl.BlockSpec(memory_space=pltpu.VMEM)] * len(kept)
        + [pl.BlockSpec(memory_space=pl.ANY)] * len(after),
        out_specs=pl.BlockSpec(memory_space=pl.ANY),
        input_output_aliases={0: 0},
        compiler_params=pltpu.CompilerParams(vmem_limit_bytes=VMEM_LIMIT),
        name="hold",
    )(value, *kept, *after)


def unit_of(ref, owner, unit):
    if unit < 4:
        return ref[2 * owner + unit // 2, :, 512 * (unit % 2) : 512 * (unit % 2) + 512]
    half = pl.ds(pl.multiple_of(512 * lax.rem(owner, 2), 512), 512)
    return ref[8 + owner // 2, :, half]


def back_kernel(places, right, own, one, two, three, keep, send, field, slots, shared):
    here = places[0]
    chunks = (own, one, two, three)
    squares = squares_of(chunks)
    for step, chunk in enumerate(chunks):
        peer = lax.rem(here + step, 4)
        slots[2 * peer] = chunk[part(0), :]
        slots[2 * peer + 1] = chunk[part(1), :]
        shared[peer] = chunk[part(2), :].astype(F32)
    slots[8] = (shared[0] + shared[1]).astype(BF)
    slots[9] = (shared[2] + shared[3]).astype(BF)
    write_partial(places, in_slots(slots), right, squares, keep, send, field)


def core_kernel(places, keep, got, out):
    both = keep[...] + got[...].astype(F32)
    out[:, 0:512] = both[:, 0:512].astype(BF)
    tail = pieces_in_rows(jnp.sum(both[0:8, 512:640], axis=0, keepdims=True))
    out[:, 512:640] = jnp.concatenate([tail] * 32, axis=0).astype(BF)


def shard_kernel(first, places, got, *refs):
    before, model_len = (None, None) if first else refs[:2]
    state, send, column = refs[0 if first else 2 :]
    total = jnp.sum(got[...].astype(F32).reshape(32, 8, 640), axis=0)
    squares = jnp.sum(total[:, 512:640], axis=0, keepdims=True)
    data_len = jnp.sqrt(squares + EPSILON)
    column[...] = jnp.broadcast_to(to_column(data_len), (64, 128))
    row = places[2]
    length = column[pl.ds(row, 1), 0:1]
    value = total[:, 0:512] / length
    if not first:
        ratio = length / model_len[pl.ds(row, 1), 0:1]
        value = value - ratio * before[0:8, :]
    state[0:8, :] = value
    state[8:16, 0:128] = jnp.broadcast_to(data_len, (8, 128))
    state[8:16, 128:512] = jnp.zeros((8, 384), F32)
    send[...] = jnp.concatenate([value] * 32, axis=0).astype(BF)


def length_column(state):
    return jnp.broadcast_to(to_column(state[8:9, 0:128]), (64, 128))


def read_model(places, mine, other, model, field):
    core = places[1]
    here = pl.ds(pl.multiple_of(256 * core, 256), 256)
    there = pl.ds(pl.multiple_of(256 * (1 - core), 256), 256)
    for i in range(4):
        field[i, here, :] = mine[:, 128 * i : 128 * i + 128].astype(F32)
        field[i, there, :] = other[:, 128 * i : 128 * i + 128].astype(F32)
    total = jnp.zeros((64, 128), F32)
    for at in range(32):
        value = field[at % 4, pl.ds(at // 4, 64, stride=8), :]
        model[:, 128 * at : 128 * at + 128] = value.astype(BF)
        total = total + value * value
    return lane_sum(total)


def forward_kernel(places, mine, other, right, model, own, one, two, three, field, slots):
    squares = read_model(places, mine, other, model, field)
    for t in range(4):
        factors = jnp.concatenate([right[pair, t] for pair in range(10)], axis=0)
        value = dot_nt(model[:, 1024 * t : 1024 * t + 1024], factors).astype(BF)
        for j in range(10):
            slots[j, :, 32 * t : 32 * t + 32] = value[:, 32 * j : 32 * j + 32]
    tail = pieces_in_rows(to_row(squares), 16).astype(BF)
    here = places[0]
    for step, chunk in enumerate((own, one, two, three)):
        peer = lax.rem(here + step, 4)
        chunk[part(0), :] = slots[2 * peer]
        chunk[part(1), :] = slots[2 * peer + 1]
        chunk[part(2), :] = slots[8 + peer // 2]
        chunk[TAIL, :] = tail


def data_kernel(last, places, *refs):
    coeffs, blocks, (left, field, state), refs = refs[:4], refs[4:7], refs[7:10], refs[10:]
    model_len, data_len, outs = refs[0], refs[1], refs[2:6]
    data_len[...] = length_column(state)
    length = jnp.sqrt(squares_of(coeffs) + EPSILON)
    model_len[...] = jnp.broadcast_to(length, (64, 128))
    inverse = 1.0 / length
    ratio = length / data_len[:, 0:1]
    total = jnp.zeros((64, 128), F32)
    for i in range(3):
        given = jnp.concatenate([chunk[part(i), :] for chunk in coeffs], axis=1)
        back = None
        for unit in range(2 * i, min(2 * i + 2, 5)):
            factors = [unit_of(left, places[0], unit)] + [block[unit] for block in blocks]
            factors = jnp.concatenate(factors, axis=0)
            value = dot(given, factors) * inverse - ratio * field[unit].astype(F32)
            if not last:
                refs[6][unit] = value
            term = dot_nt(value.astype(BF), factors)
            back = term if back is None else back + term
            value = value * value
            total = total + sum(value[:, 128 * k : 128 * k + 128] for k in range(4))
        back = back.astype(BF)
        for step in range(4):
            outs[step][part(i), :] = back[:, 128 * step : 128 * step + 128]
    tail = pieces_in_rows(to_row(lane_sum(total)), 16).astype(BF)
    for step in range(4):
        outs[step][TAIL, :] = tail


def last_model_kernel(places, mine, other, state, model, data_len, squares, field):
    data_len[...] = length_column(state)
    squares[...] = jnp.broadcast_to(
        read_model(places, mine, other, model, field), (64, 128)
    )


def scalars(data_lens, model_lens):
    diagonal_bar, residual = model_lens[0], data_lens[0]
    out = []
    for sweep in range(ITERS):
        data_len = data_lens[sweep + 1]
        rotation = jnp.sqrt(diagonal_bar * diagonal_bar + data_len * data_len)
        cosine_term = diagonal_bar / rotation
        sine_term = data_len / rotation
        into_solution = (cosine_term * residual) / rotation
        residual = sine_term * residual
        into_direction = None
        if sweep + 1 < len(model_lens):
            into_direction = (sine_term * model_lens[sweep + 1]) / rotation
            diagonal_bar = -cosine_term * model_lens[sweep + 1]
        out.append((into_solution, into_direction))
    return out, residual


def solution_kernel(places, *refs):
    data_lens, model_lens, (first, second) = refs[:3], refs[3:5], refs[5:7]
    solved, residual_estimate, last_direction = refs[7:]
    model_lens = [ref[:, 0:1] for ref in model_lens]
    steps, residual = scalars([ref[:, 0:1] for ref in data_lens], model_lens)
    residual_estimate[...] = jnp.broadcast_to(residual, (64, 128))
    for t in range(4):
        part = slice(1024 * t, 1024 * t + 1024)
        direction = first[:, part].astype(F32) / model_lens[0]
        value = steps[0][0] * direction
        direction = second[:, part].astype(F32) / model_lens[1] - steps[0][1] * direction
        solved[t] = value + steps[1][0] * direction
        last_direction[t] = direction


def direction_kernel(places, *refs):
    data_lens, model_lens, squares = refs[:3], refs[3:5], refs[5:9]
    third, last_direction, out, made, sems = refs[9:]
    copies = [pltpu.make_async_copy(made.at[t], out.at[t], sems.at[t]) for t in range(4)]
    length = jnp.sqrt(sum(ref[:, 0:1] for ref in squares) + EPSILON)
    model_lens = [ref[:, 0:1] for ref in model_lens] + [length]
    steps, residual = scalars([ref[:, 0:1] for ref in data_lens], model_lens)
    for t in range(4):
        model = third[:, 1024 * t : 1024 * t + 1024].astype(F32) / length
        made[t] = model - steps[1][1] * last_direction[t]
        copies[t].start()
    for copy in copies:
        copy.wait()


def shift(value, step):
    return lax.ppermute(value, "x", [(i, (i + step) % 4) for i in range(4)])


def swap_core(value):
    return lax.ppermute(value, "c", [(0, 1), (1, 0)])


def exchange(value):
    width = value.shape[1]
    value = lax.all_to_all(
        value.reshape(32, 8, width), ("z", "y"), split_axis=0, concat_axis=0, tiled=True
    )
    return value.reshape(256, width)


PARTIAL = [((256, 640), F32), ((256, 640), BF)]
PARTIAL_SCRATCH = [((4, 512, 128), F32), ((10, 64, 128), BF)]
CHUNKS = [((208, 128), BF)] * 4
COLUMN = ((64, 128), F32)
MODEL = ((64, 4096), BF)


def on_device(left, right, observations):
    left = left.reshape(10, 128, 1024)
    right = right.reshape(10, 4, 32, 1024)
    observations = observations.reshape(10, 64, 1024)

    def sum_dp(whole, extra, before_gather=()):
        state, send = call(
            functools.partial(shard_kernel, not extra),
            [((16, 512), F32), ((256, 512), BF)],
            [COLUMN],
            name="shard",
        )(exchange(whole), *extra)
        mine = exchange(send)
        if before_gather:
            mine = hold(mine, (), before_gather)
        return state, mine, swap_core(mine)

    one, two, three = call(pack_kernel, [((5, 128, 512), BF)] * 3, name="pack")(left)
    slots, squares, own_field = call(
        start_kernel,
        [((10, 64, 128), BF), COLUMN, ((5, 64, 512), BF)],
        name="start",
        after=(one, two, three),
    )(left, observations)
    keep, send = call(first_back_kernel, PARTIAL, PARTIAL_SCRATCH[:1], name="start_sum")(
        right, slots, squares
    )
    one, three = shift(one, 1), shift(three, 3)
    two = shift(hold(two, (right,), (one, three)), 2)
    blocks = [one, two, three]
    whole = call(core_kernel, [((256, 640), BF)], name="core_sum")(
        keep, swap_core(send)
    )[0]
    state, mine, other = sum_dp(whole, (), (two,))
    field = own_field
    models, model_lens, data_lens = [], [], []
    for sweep in range(ITERS):
        model, *chunks = call(
            forward_kernel,
            [MODEL] + CHUNKS,
            [((4, 512, 128), F32), ((10, 64, 128), BF)],
            name="forward",
        )(mine, other, right)
        models.append(model)
        chunks = [chunks[0]] + [shift(chunks[step], step) for step in (1, 2, 3)]
        last = sweep == ITERS - 1
        outs = call(
            functools.partial(data_kernel, last),
            [COLUMN, COLUMN] + CHUNKS + ([] if last else [((5, 64, 512), F32)]),
            name="data",
        )(*chunks, *blocks, left, field, state)
        model_lens.append(outs[0])
        data_lens.append(outs[1])
        field = None if last else outs[6]
        chunks = [outs[2]] + [shift(outs[2 + step], -step) for step in (1, 2, 3)]
        keep, send = call(
            back_kernel, PARTIAL, PARTIAL_SCRATCH + [((4, 64, 128), F32)], name="back"
        )(right, *chunks)
        whole = call(core_kernel, [((256, 640), BF)], name="core_sum")(
            keep, swap_core(send)
        )[0]
        state, mine, other = sum_dp(whole, (state, model_lens[-1]))

    model, data_len, squares = call(
        last_model_kernel,
        [MODEL, COLUMN, COLUMN],
        [((4, 512, 128), F32)],
        name="last_model",
    )(mine, other, state)
    data_lens.append(data_len)
    solve_after = (squares,)
    squares = [squares] + [shift(squares, step) for step in (1, 2, 3)]
    solved, residual, last_direction = call(
        solution_kernel,
        [((4, 64, 1024), F32), COLUMN, ((4, 64, 1024), F32)],
        name="solve",
        after=solve_after,
    )(*data_lens, *model_lens, *models)
    direction = call(
        direction_kernel,
        [((4, 64, 1024), F32)],
        [((4, 64, 1024), F32), pltpu.SemaphoreType.DMA((4,))],
        name="direct",
        out_space=pl.ANY,
    )(
        *data_lens, *model_lens, *squares, model, last_direction
    )[0]
    return solved, direction, residual[:, 0]


def solution(mesh):
    fine = Mesh(mesh.devices.reshape(8, 4, 2, 4), ("z", "y", "c", "x"))
    rows = ("z", "y", "c")
    return jax.shard_map(
        on_device,
        mesh=fine,
        in_specs=(
            P(rows, None, "x", None, None),
            P(rows, None, "x", None, None),
            P(rows, None, None, None),
        ),
        out_specs=(P("x", None, None), P("x", None, None), P()),
        check_vma=False,
    )
```

```python
import functools

import jax
import jax.numpy as jnp
from jax import lax
from jax.experimental import pallas as pl
from jax.experimental.pallas import tpu as pltpu
from jax.sharding import Mesh
from jax.sharding import PartitionSpec as P

ITERS = 2
EPSILON = 1e-06
BF = jnp.bfloat16
F32 = jnp.float32
VMEM_LIMIT = 20 * 1024 * 1024


def call(kernel, outs, scratch=(), name=None, after=()):
    given = kernel

    def run(*operands):
        count = len(operands)

        def kernel(*refs):
            core = lax.axis_index("c")
            row = 32 * core + 4 * lax.axis_index("z") + lax.axis_index("y")
            places = (lax.axis_index("x"), core, row)
            given(places, *refs[:count], *refs[count + len(after) :])

        return pl.pallas_call(
            kernel,
            out_shape=[jax.ShapeDtypeStruct(out[0], out[1]) for out in outs],
            in_specs=[pl.BlockSpec(memory_space=pltpu.VMEM)] * len(operands)
            + [pl.BlockSpec(memory_space=pl.ANY)] * len(after),
            out_specs=[pl.BlockSpec(memory_space=pltpu.VMEM)] * len(outs),
            scratch_shapes=[
                pltpu.VMEM(*entry) if isinstance(entry, tuple) else entry
                for entry in scratch
            ],
            compiler_params=pltpu.CompilerParams(vmem_limit_bytes=VMEM_LIMIT),
            name=name,
        )(*operands, *after)

    return run


def dot(first, second):
    return jnp.dot(first, second, preferred_element_type=F32)


def dot_nt(first, second):
    return lax.dot_general(
        first, second, (((1,), (1,)), ((), ())), preferred_element_type=F32
    )


def split(value):
    first = value.astype(BF).astype(F32)
    rest = value - first
    second = rest.astype(BF).astype(F32)
    return first, second, (rest - second).astype(BF).astype(F32)


def lane_sum(value):
    return jnp.sum(value, axis=-1, keepdims=True)


def pieces_in_rows(row, count=8):
    first, second, third = split(row)
    at = lax.broadcasted_iota(jnp.int32, (count, 128), 0)
    return jnp.where(
        at == 0, first, jnp.where(at == 1, second, jnp.where(at == 2, third, 0.0))
    )


def part(index):
    return pl.ds(64 * index, 64)


TAIL = pl.ds(192, 16)


def squares_of(chunks):
    total = sum(chunk[TAIL, :].astype(F32) for chunk in chunks)
    return jnp.sum(total, axis=0, keepdims=True)


def diagonal():
    return lax.broadcasted_iota(jnp.int32, (64, 128), 0) == lax.broadcasted_iota(
        jnp.int32, (64, 128), 1
    )


def to_row(column):
    return jnp.sum(jnp.where(diagonal(), column, 0.0), axis=0, keepdims=True)


def to_column(row):
    return lane_sum(jnp.where(diagonal(), row, 0.0))


def write_partial(places, coeffs, right, squares, keep, send, field):
    for t in range(4):
        factors = jnp.concatenate([right[pair, t] for pair in range(10)], axis=0)
        value = dot(coeffs(t), factors)
        for i in range(8):
            field[i % 4, pl.ds(2 * t + i // 4, 64, stride=8), :] = value[
                :, 128 * i : 128 * i + 128
            ]
    core = places[1]
    kept = pl.ds(pl.multiple_of(256 * core, 256), 256)
    sent = pl.ds(pl.multiple_of(256 * (1 - core), 256), 256)
    for i in range(4):
        keep[:, 128 * i : 128 * i + 128] = field[i, kept, :]
        send[:, 128 * i : 128 * i + 128] = field[i, sent, :].astype(BF)
    tail = jnp.concatenate([pieces_in_rows(squares)] * 32, axis=0)
    keep[:, 512:640] = tail
    send[:, 512:640] = tail.astype(BF)


def in_slots(slots):
    return lambda t: jnp.concatenate(
        [slots[j][:, 32 * t : 32 * t + 32] for j in range(10)], axis=1
    )


def start_kernel(places, left, observations, slots, squares, own_field):
    for unit in range(5):
        own_field[unit] = unit_of(observations, places[0], unit)
    total = jnp.zeros((64, 128), F32)
    for pair in range(10):
        values = observations[pair]
        wide = values.astype(F32)
        wide = wide * wide
        total = total + sum(wide[:, 128 * i : 128 * i + 128] for i in range(8))
        slots[pair] = dot_nt(values, left[pair]).astype(BF)
    squares[...] = jnp.broadcast_to(to_row(lane_sum(total)), (8, 128))


def first_back_kernel(places, right, slots, squares, keep, send, field):
    write_partial(places, in_slots(slots), right, squares[0:1, :], keep, send, field)


def pack_kernel(places, left, one, two, three):
    here = places[0]
    for unit in range(5):
        for step, out in ((1, one), (2, two), (3, three)):
            out[unit] = unit_of(left, lax.rem(here + step, 4), unit)


def hold(value, kept=(), after=()):
    return pl.pallas_call(
        lambda *refs: None,
        out_shape=jax.ShapeDtypeStruct(value.shape, value.dtype),
        in_specs=[pl.BlockSpec(memory_space=pl.ANY)]
        + [pl.BlockSpec(memory_space=pltpu.VMEM)] * len(kept)
        + [pl.BlockSpec(memory_space=pl.ANY)] * len(after),
        out_specs=pl.BlockSpec(memory_space=pl.ANY),
        input_output_aliases={0: 0},
        compiler_params=pltpu.CompilerParams(vmem_limit_bytes=VMEM_LIMIT),
        name="hold",
    )(value, *kept, *after)


def unit_of(ref, owner, unit):
    if unit < 4:
        return ref[2 * owner + unit // 2, :, 512 * (unit % 2) : 512 * (unit % 2) + 512]
    half = pl.ds(pl.multiple_of(512 * lax.rem(owner, 2), 512), 512)
    return ref[8 + owner // 2, :, half]


def back_kernel(places, right, own, one, two, three, keep, send, field, slots, shared):
    here = places[0]
    chunks = (own, one, two, three)
    squares = squares_of(chunks)
    for step, chunk in enumerate(chunks):
        peer = lax.rem(here + step, 4)
        slots[2 * peer] = chunk[part(0), :]
        slots[2 * peer + 1] = chunk[part(1), :]
        shared[peer] = chunk[part(2), :].astype(F32)
    slots[8] = (shared[0] + shared[1]).astype(BF)
    slots[9] = (shared[2] + shared[3]).astype(BF)
    write_partial(places, in_slots(slots), right, squares, keep, send, field)


def core_kernel(places, keep, got, out):
    both = keep[...] + got[...].astype(F32)
    out[:, 0:512] = both[:, 0:512].astype(BF)
    tail = pieces_in_rows(jnp.sum(both[0:8, 512:640], axis=0, keepdims=True))
    out[:, 512:640] = jnp.concatenate([tail] * 32, axis=0).astype(BF)


def shard_kernel(first, places, got, *refs):
    before, model_len = (None, None) if first else refs[:2]
    state, send = refs[0 if first else 2 :]
    total = jnp.sum(got[...].astype(F32).reshape(32, 8, 640), axis=0)
    squares = jnp.sum(total[:, 512:640], axis=0, keepdims=True)
    data_len = jnp.sqrt(squares + EPSILON)
    row = places[2]
    at = lax.broadcasted_iota(jnp.int32, (1, 128), 1)
    length = lane_sum(jnp.where(at == row, data_len, 0.0))
    value = total[:, 0:512] / length
    if not first:
        ratio = length / model_len[pl.ds(row, 1), 0:1]
        value = value - ratio * before[0:8, :]
    state[0:8, :] = value
    state[8:16, 0:128] = jnp.broadcast_to(data_len, (8, 128))
    state[8:16, 128:512] = jnp.zeros((8, 384), F32)
    send[...] = jnp.concatenate([value] * 32, axis=0).astype(BF)


def length_column(state):
    return jnp.broadcast_to(to_column(state[8:9, 0:128]), (64, 128))


def read_model(places, mine, other, model, field):
    core = places[1]
    here = pl.ds(pl.multiple_of(256 * core, 256), 256)
    there = pl.ds(pl.multiple_of(256 * (1 - core), 256), 256)
    for i in range(4):
        field[i, here, :] = mine[:, 128 * i : 128 * i + 128].astype(F32)
        field[i, there, :] = other[:, 128 * i : 128 * i + 128].astype(F32)
    total = jnp.zeros((64, 128), F32)
    for at in range(32):
        value = field[at % 4, pl.ds(at // 4, 64, stride=8), :]
        model[:, 128 * at : 128 * at + 128] = value.astype(BF)
        total = total + value * value
    return lane_sum(total)


def forward_kernel(places, mine, other, right, model, own, one, two, three, field, slots):
    squares = read_model(places, mine, other, model, field)
    for t in range(4):
        factors = jnp.concatenate([right[pair, t] for pair in range(10)], axis=0)
        value = dot_nt(model[:, 1024 * t : 1024 * t + 1024], factors).astype(BF)
        for j in range(10):
            slots[j, :, 32 * t : 32 * t + 32] = value[:, 32 * j : 32 * j + 32]
    tail = pieces_in_rows(to_row(squares), 16).astype(BF)
    here = places[0]
    for step, chunk in enumerate((own, one, two, three)):
        peer = lax.rem(here + step, 4)
        chunk[part(0), :] = slots[2 * peer]
        chunk[part(1), :] = slots[2 * peer + 1]
        chunk[part(2), :] = slots[8 + peer // 2]
        chunk[TAIL, :] = tail


def data_kernel(last, places, *refs):
    coeffs, refs = refs[:4], refs[4:]
    (field, state, units), refs = (refs[:3], refs[3:]) if last else ((*refs[:2], refs[-1]), refs[2:])
    if not last:
        blocks, refs = refs[:4], refs[4:]
        for unit in range(5):
            units[unit, 0:128, :] = unit_of(blocks[0], places[0], unit)
            for step in (1, 2, 3):
                units[unit, 128 * step : 128 * step + 128, :] = blocks[step][unit]
    model_len, data_len, outs = refs[0], refs[1], refs[2:6]
    data_len[...] = length_column(state)
    length = to_column(jnp.sqrt(squares_of(coeffs) + EPSILON))
    model_len[...] = jnp.broadcast_to(length, (64, 128))
    inverse = 1.0 / length
    ratio = length / data_len[:, 0:1]
    total = jnp.zeros((64, 128), F32)
    for i in range(3):
        given = jnp.concatenate([chunk[part(i), :] for chunk in coeffs], axis=1)
        back = None
        for unit in range(2 * i, min(2 * i + 2, 5)):
            factors = units[unit]
            value = dot(given, factors) * inverse - ratio * field[unit].astype(F32)
            if not last:
                refs[6][unit] = value
            term = dot_nt(value.astype(BF), factors)
            back = term if back is None else back + term
            value = value * value
            total = total + sum(value[:, 128 * k : 128 * k + 128] for k in range(4))
        back = back.astype(BF)
        for step in range(4):
            outs[step][part(i), :] = back[:, 128 * step : 128 * step + 128]
    tail = pieces_in_rows(to_row(lane_sum(total)), 16).astype(BF)
    for step in range(4):
        outs[step][TAIL, :] = tail


def last_model_kernel(places, mine, other, state, model, data_len, squares, field):
    data_len[...] = length_column(state)
    total = to_row(read_model(places, mine, other, model, field))
    squares[...] = jnp.broadcast_to(total, (8, 128))


def scalars(data_lens, model_lens):
    diagonal_bar, residual = model_lens[0], data_lens[0]
    out = []
    for sweep in range(ITERS):
        data_len = data_lens[sweep + 1]
        rotation = jnp.sqrt(diagonal_bar * diagonal_bar + data_len * data_len)
        cosine_term = diagonal_bar / rotation
        sine_term = data_len / rotation
        into_solution = (cosine_term * residual) / rotation
        residual = sine_term * residual
        into_direction = None
        if sweep + 1 < len(model_lens):
            into_direction = (sine_term * model_lens[sweep + 1]) / rotation
            diagonal_bar = -cosine_term * model_lens[sweep + 1]
        out.append((into_solution, into_direction))
    return out, residual


def solution_kernel(places, *refs):
    data_lens, model_lens, (first, second) = refs[:3], refs[3:5], refs[5:7]
    solved, residual_estimate, last_direction = refs[7:]
    model_lens = [ref[:, 0:1] for ref in model_lens]
    steps, residual = scalars([ref[:, 0:1] for ref in data_lens], model_lens)
    residual_estimate[...] = jnp.broadcast_to(residual, (64, 128))
    for t in range(4):
        part = slice(1024 * t, 1024 * t + 1024)
        direction = first[:, part].astype(F32) / model_lens[0]
        value = steps[0][0] * direction
        direction = second[:, part].astype(F32) / model_lens[1] - steps[0][1] * direction
        solved[t] = value + steps[1][0] * direction
        last_direction[t] = direction


def direction_kernel(places, *refs):
    data_lens, model_lens, squares = refs[:3], refs[3:5], refs[5:9]
    third, last_direction, out = refs[9:]
    squares = sum(ref[0:1, :] for ref in squares)
    length = jnp.sqrt(to_column(squares) + EPSILON)
    model_lens = [ref[:, 0:1] for ref in model_lens] + [length]
    steps, residual = scalars([ref[:, 0:1] for ref in data_lens], model_lens)
    for t in range(4):
        model = third[:, 1024 * t : 1024 * t + 1024].astype(F32) / length
        out[t] = model - steps[1][1] * last_direction[t]


def shift(value, step):
    return lax.ppermute(value, "x", [(i, (i + step) % 4) for i in range(4)])


def swap_core(value):
    return lax.ppermute(value, "c", [(0, 1), (1, 0)])


def exchange(value):
    width = value.shape[1]
    value = lax.all_to_all(
        value.reshape(32, 8, width), ("z", "y"), split_axis=0, concat_axis=0, tiled=True
    )
    return value.reshape(256, width)


PARTIAL = [((256, 640), F32), ((256, 640), BF)]
PARTIAL_SCRATCH = [((4, 512, 128), F32), ((10, 64, 128), BF)]
CHUNKS = [((208, 128), BF)] * 4
COLUMN = ((64, 128), F32)
MODEL = ((64, 4096), BF)


def on_device(left, right, observations):
    left = left.reshape(10, 128, 1024)
    right = right.reshape(10, 4, 32, 1024)
    observations = observations.reshape(10, 64, 1024)

    def sum_dp(whole, extra, before_gather=()):
        state, send = call(
            functools.partial(shard_kernel, not extra),
            [((16, 512), F32), ((256, 512), BF)],
            name="shard",
        )(exchange(whole), *extra)
        mine = exchange(send)
        if before_gather:
            mine = hold(mine, (), before_gather)
        return state, mine, swap_core(mine)

    one, two, three = call(pack_kernel, [((5, 128, 512), BF)] * 3, name="pack")(left)
    slots, squares, own_field = call(
        start_kernel,
        [((10, 64, 128), BF), ((8, 128), F32), ((5, 64, 512), BF)],
        name="start",
        after=(one, two, three),
    )(left, observations)
    keep, send = call(first_back_kernel, PARTIAL, PARTIAL_SCRATCH[:1], name="start_sum")(
        right, slots, squares
    )
    one, three = shift(one, 1), shift(three, 3)
    two = shift(hold(two, (right,), (one, three)), 2)
    blocks = [one, two, three]
    whole = call(core_kernel, [((256, 640), BF)], name="core_sum")(
        keep, swap_core(send)
    )[0]
    state, mine, other = sum_dp(whole, (), (two,))
    field, factors = own_field, (left, *blocks)
    models, model_lens, data_lens = [], [], []
    for sweep in range(ITERS):
        model, *chunks = call(
            forward_kernel,
            [MODEL] + CHUNKS,
            [((4, 512, 128), F32), ((10, 64, 128), BF)],
            name="forward",
        )(mine, other, right)
        models.append(model)
        chunks = [chunks[0]] + [shift(chunks[step], step) for step in (1, 2, 3)]
        last = sweep == ITERS - 1
        outs = call(
            functools.partial(data_kernel, last),
            [COLUMN, COLUMN]
            + CHUNKS
            + ([] if last else [((5, 64, 512), F32), ((5, 512, 512), BF)]),
            name="data",
        )(*chunks, field, state, *factors)
        model_lens.append(outs[0])
        data_lens.append(outs[1])
        field, factors = (None, None) if last else (outs[6], outs[7:])
        chunks = [outs[2]] + [shift(outs[2 + step], -step) for step in (1, 2, 3)]
        keep, send = call(
            back_kernel, PARTIAL, PARTIAL_SCRATCH + [((4, 64, 128), F32)], name="back"
        )(right, *chunks)
        whole = call(core_kernel, [((256, 640), BF)], name="core_sum")(
            keep, swap_core(send)
        )[0]
        state, mine, other = sum_dp(whole, (state, model_lens[-1]))

    model, data_len, squares = call(
        last_model_kernel,
        [MODEL, COLUMN, ((8, 128), F32)],
        [((4, 512, 128), F32)],
        name="last_model",
    )(mine, other, state)
    data_lens.append(data_len)
    solve_after = (squares,)
    squares = [squares] + [shift(squares, step) for step in (1, 2, 3)]
    solved, residual, last_direction = call(
        solution_kernel,
        [((4, 64, 1024), F32), COLUMN, ((4, 64, 1024), F32)],
        name="solve",
        after=solve_after,
    )(*data_lens, *model_lens, *models)
    direction = call(direction_kernel, [((4, 64, 1024), F32)], name="direct")(
        *data_lens, *model_lens, *squares, model, last_direction
    )[0]
    return solved, direction, residual[:, 0]


def solution(mesh):
    fine = Mesh(mesh.devices.reshape(8, 4, 2, 4), ("z", "y", "c", "x"))
    rows = ("z", "y", "c")
    return jax.shard_map(
        on_device,
        mesh=fine,
        in_specs=(
            P(rows, None, "x", None, None),
            P(rows, None, "x", None, None),
            P(rows, None, None, None),
        ),
        out_specs=(P("x", None, None), P("x", None, None), P()),
        check_vma=False,
    )
```

```python
import functools

import jax
import jax.numpy as jnp
from jax import lax
from jax.experimental import pallas as pl
from jax.experimental.pallas import tpu as pltpu
from jax.sharding import Mesh
from jax.sharding import PartitionSpec as P

ITERS = 2
EPSILON = 1e-06
BF = jnp.bfloat16
F32 = jnp.float32
VMEM_LIMIT = 20 * 1024 * 1024


def call(kernel, outs, scratch=(), name=None, after=(), anywhere=False):
    given = kernel

    def run(*operands):
        count = len(operands)

        def kernel(*refs):
            core = lax.axis_index("c")
            row = 32 * core + 4 * lax.axis_index("z") + lax.axis_index("y")
            places = (lax.axis_index("x"), core, row)
            given(places, *refs[:count], *refs[count + len(after) :])

        return pl.pallas_call(
            kernel,
            out_shape=[jax.ShapeDtypeStruct(out[0], out[1]) for out in outs],
            in_specs=[pl.BlockSpec(memory_space=pl.ANY if anywhere else pltpu.VMEM)]
            * len(operands)
            + [pl.BlockSpec(memory_space=pl.ANY)] * len(after),
            out_specs=[pl.BlockSpec(memory_space=pltpu.VMEM)] * len(outs),
            scratch_shapes=[
                pltpu.VMEM(*entry) if isinstance(entry, tuple) else entry
                for entry in scratch
            ],
            compiler_params=pltpu.CompilerParams(vmem_limit_bytes=VMEM_LIMIT),
            name=name,
        )(*operands, *after)

    return run


def dot(first, second):
    return jnp.dot(first, second, preferred_element_type=F32)


def dot_nt(first, second):
    return lax.dot_general(
        first, second, (((1,), (1,)), ((), ())), preferred_element_type=F32
    )


def split(value):
    first = value.astype(BF).astype(F32)
    rest = value - first
    second = rest.astype(BF).astype(F32)
    return first, second, (rest - second).astype(BF).astype(F32)


def lane_sum(value):
    return jnp.sum(value, axis=-1, keepdims=True)


def pieces_in_rows(row, count=8):
    first, second, third = split(row)
    at = lax.broadcasted_iota(jnp.int32, (count, 128), 0)
    return jnp.where(
        at == 0, first, jnp.where(at == 1, second, jnp.where(at == 2, third, 0.0))
    )


def part(index):
    return pl.ds(64 * index, 64)


TAIL = pl.ds(192, 16)


def squares_of(chunks):
    total = sum(chunk[TAIL, :].astype(F32) for chunk in chunks)
    return jnp.sum(total, axis=0, keepdims=True)


def diagonal():
    return lax.broadcasted_iota(jnp.int32, (64, 128), 0) == lax.broadcasted_iota(
        jnp.int32, (64, 128), 1
    )


def to_row(column):
    return jnp.sum(jnp.where(diagonal(), column, 0.0), axis=0, keepdims=True)


def to_column(row):
    return lane_sum(jnp.where(diagonal(), row, 0.0))


def write_partial(places, coeffs, right, squares, keep, send, field):
    for t in range(4):
        factors = jnp.concatenate([right[pair, t] for pair in range(10)], axis=0)
        value = dot(coeffs(t), factors)
        for i in range(8):
            field[i % 4, pl.ds(2 * t + i // 4, 64, stride=8), :] = value[
                :, 128 * i : 128 * i + 128
            ]
    core = places[1]
    kept = pl.ds(pl.multiple_of(256 * core, 256), 256)
    sent = pl.ds(pl.multiple_of(256 * (1 - core), 256), 256)
    for i in range(4):
        keep[:, 128 * i : 128 * i + 128] = field[i, kept, :]
        send[:, 128 * i : 128 * i + 128] = field[i, sent, :].astype(BF)
    tail = jnp.concatenate([pieces_in_rows(squares)] * 32, axis=0)
    keep[:, 512:640] = tail
    send[:, 512:640] = tail.astype(BF)


def in_slots(slots):
    return lambda t: jnp.concatenate(
        [slots[j][:, 32 * t : 32 * t + 32] for j in range(10)], axis=1
    )


def start_kernel(places, left, observations, slots, squares, own_field):
    for unit in range(5):
        own_field[unit] = unit_of(observations, places[0], unit)
    total = jnp.zeros((64, 128), F32)
    for pair in range(10):
        values = observations[pair]
        wide = values.astype(F32)
        wide = wide * wide
        total = total + sum(wide[:, 128 * i : 128 * i + 128] for i in range(8))
        slots[pair] = dot_nt(values, left[pair]).astype(BF)
    squares[...] = jnp.broadcast_to(to_row(lane_sum(total)), (8, 128))


def first_back_kernel(places, right, slots, squares, keep, send, field):
    write_partial(places, in_slots(slots), right, squares[0:1, :], keep, send, field)


def pack_kernel(places, left, one, two, three):
    here = places[0]
    for unit in range(5):
        for step, out in ((1, one), (2, two), (3, three)):
            out[unit] = unit_of(left, lax.rem(here + step, 4), unit)


def hold(value, kept=(), after=()):
    return pl.pallas_call(
        lambda *refs: None,
        out_shape=jax.ShapeDtypeStruct(value.shape, value.dtype),
        in_specs=[pl.BlockSpec(memory_space=pl.ANY)]
        + [pl.BlockSpec(memory_space=pltpu.VMEM)] * len(kept)
        + [pl.BlockSpec(memory_space=pl.ANY)] * len(after),
        out_specs=pl.BlockSpec(memory_space=pl.ANY),
        input_output_aliases={0: 0},
        compiler_params=pltpu.CompilerParams(vmem_limit_bytes=VMEM_LIMIT),
        name="hold",
    )(value, *kept, *after)


def unit_of(ref, owner, unit):
    if unit < 4:
        return ref[2 * owner + unit // 2, :, 512 * (unit % 2) : 512 * (unit % 2) + 512]
    half = pl.ds(pl.multiple_of(512 * lax.rem(owner, 2), 512), 512)
    return ref[8 + owner // 2, :, half]


def back_kernel(places, right, own, one, two, three, keep, send, field, slots, shared):
    here = places[0]
    chunks = (own, one, two, three)
    squares = squares_of(chunks)
    for step, chunk in enumerate(chunks):
        peer = lax.rem(here + step, 4)
        slots[2 * peer] = chunk[part(0), :]
        slots[2 * peer + 1] = chunk[part(1), :]
        shared[peer] = chunk[part(2), :].astype(F32)
    slots[8] = (shared[0] + shared[1]).astype(BF)
    slots[9] = (shared[2] + shared[3]).astype(BF)
    write_partial(places, in_slots(slots), right, squares, keep, send, field)


def core_kernel(places, keep, got, out):
    both = keep[...] + got[...].astype(F32)
    out[:, 0:512] = both[:, 0:512].astype(BF)
    tail = pieces_in_rows(jnp.sum(both[0:8, 512:640], axis=0, keepdims=True))
    out[:, 512:640] = jnp.concatenate([tail] * 32, axis=0).astype(BF)


def shard_kernel(first, places, got, *refs):
    before, model_len = (None, None) if first else refs[:2]
    state, send = refs[0 if first else 2 :]
    total = jnp.sum(got[...].astype(F32).reshape(32, 8, 640), axis=0)
    squares = jnp.sum(total[:, 512:640], axis=0, keepdims=True)
    data_len = jnp.sqrt(squares + EPSILON)
    row = places[2]
    at = lax.broadcasted_iota(jnp.int32, (1, 128), 1)
    length = lane_sum(jnp.where(at == row, data_len, 0.0))
    value = total[:, 0:512] / length
    if not first:
        ratio = length / model_len[pl.ds(row, 1), 0:1]
        value = value - ratio * before[0:8, :]
    state[0:8, :] = value
    state[8:16, 0:128] = jnp.broadcast_to(data_len, (8, 128))
    state[8:16, 128:512] = jnp.zeros((8, 384), F32)
    send[...] = jnp.concatenate([value] * 32, axis=0).astype(BF)


def length_column(state):
    return jnp.broadcast_to(to_column(state[8:9, 0:128]), (64, 128))


def read_model(places, mine, other, model, field):
    core = places[1]
    here = pl.ds(pl.multiple_of(256 * core, 256), 256)
    there = pl.ds(pl.multiple_of(256 * (1 - core), 256), 256)
    for i in range(4):
        field[i, here, :] = mine[:, 128 * i : 128 * i + 128].astype(F32)
        field[i, there, :] = other[:, 128 * i : 128 * i + 128].astype(F32)
    total = jnp.zeros((64, 128), F32)
    for at in range(32):
        value = field[at % 4, pl.ds(at // 4, 64, stride=8), :]
        model[:, 128 * at : 128 * at + 128] = value.astype(BF)
        total = total + value * value
    return lane_sum(total)


def forward_kernel(places, mine, other, right, model, own, one, two, three, field, slots):
    squares = read_model(places, mine, other, model, field)
    for t in range(4):
        factors = jnp.concatenate([right[pair, t] for pair in range(10)], axis=0)
        value = dot_nt(model[:, 1024 * t : 1024 * t + 1024], factors).astype(BF)
        for j in range(10):
            slots[j, :, 32 * t : 32 * t + 32] = value[:, 32 * j : 32 * j + 32]
    tail = pieces_in_rows(to_row(squares), 16).astype(BF)
    here = places[0]
    for step, chunk in enumerate((own, one, two, three)):
        peer = lax.rem(here + step, 4)
        chunk[part(0), :] = slots[2 * peer]
        chunk[part(1), :] = slots[2 * peer + 1]
        chunk[part(2), :] = slots[8 + peer // 2]
        chunk[TAIL, :] = tail


def fetch_kernel(places, two, three, two_here, three_here, sems):
    copies = [
        pltpu.make_async_copy(source, target, sems.at[at])
        for at, (source, target) in enumerate(((two, two_here), (three, three_here)))
    ]
    for copy in copies:
        copy.start()
    for copy in copies:
        copy.wait()


def data_kernel(last, places, *refs):
    coeffs, refs = refs[:4], refs[4:]
    (field, state, units), refs = (refs[:3], refs[3:]) if last else ((*refs[:2], refs[-1]), refs[2:])
    if not last:
        blocks, refs = refs[:4], refs[4:]
        for unit in range(5):
            units[unit, 0:128, :] = unit_of(blocks[0], places[0], unit)
            for step in (1, 2, 3):
                units[unit, 128 * step : 128 * step + 128, :] = blocks[step][unit]
    model_len, data_len, outs = refs[0], refs[1], refs[2:6]
    data_len[...] = length_column(state)
    length = to_column(jnp.sqrt(squares_of(coeffs) + EPSILON))
    model_len[...] = jnp.broadcast_to(length, (64, 128))
    inverse = 1.0 / length
    ratio = length / data_len[:, 0:1]
    total = jnp.zeros((64, 128), F32)
    for i in range(3):
        given = jnp.concatenate([chunk[part(i), :] for chunk in coeffs], axis=1)
        back = None
        for unit in range(2 * i, min(2 * i + 2, 5)):
            factors = units[unit]
            value = dot(given, factors) * inverse - ratio * field[unit].astype(F32)
            if not last:
                refs[6][unit] = value
            term = dot_nt(value.astype(BF), factors)
            back = term if back is None else back + term
            value = value * value
            total = total + sum(value[:, 128 * k : 128 * k + 128] for k in range(4))
        back = back.astype(BF)
        for step in range(4):
            outs[step][part(i), :] = back[:, 128 * step : 128 * step + 128]
    tail = pieces_in_rows(to_row(lane_sum(total)), 16).astype(BF)
    for step in range(4):
        outs[step][TAIL, :] = tail


def last_model_kernel(places, mine, other, state, model, data_len, squares, field):
    data_len[...] = length_column(state)
    total = to_row(read_model(places, mine, other, model, field))
    squares[...] = jnp.broadcast_to(total, (8, 128))


def scalars(data_lens, model_lens):
    diagonal_bar, residual = model_lens[0], data_lens[0]
    out = []
    for sweep in range(ITERS):
        data_len = data_lens[sweep + 1]
        rotation = jnp.sqrt(diagonal_bar * diagonal_bar + data_len * data_len)
        cosine_term = diagonal_bar / rotation
        sine_term = data_len / rotation
        into_solution = (cosine_term * residual) / rotation
        residual = sine_term * residual
        into_direction = None
        if sweep + 1 < len(model_lens):
            into_direction = (sine_term * model_lens[sweep + 1]) / rotation
            diagonal_bar = -cosine_term * model_lens[sweep + 1]
        out.append((into_solution, into_direction))
    return out, residual


def solution_kernel(places, *refs):
    data_lens, model_lens, (first, second) = refs[:3], refs[3:5], refs[5:7]
    solved, residual_estimate, last_direction = refs[7:]
    model_lens = [ref[:, 0:1] for ref in model_lens]
    steps, residual = scalars([ref[:, 0:1] for ref in data_lens], model_lens)
    residual_estimate[...] = jnp.broadcast_to(residual, (64, 128))
    for t in range(4):
        part = slice(1024 * t, 1024 * t + 1024)
        direction = first[:, part].astype(F32) / model_lens[0]
        value = steps[0][0] * direction
        direction = second[:, part].astype(F32) / model_lens[1] - steps[0][1] * direction
        solved[t] = value + steps[1][0] * direction
        last_direction[t] = direction


def direction_kernel(places, *refs):
    data_lens, model_lens, squares = refs[:3], refs[3:5], refs[5:9]
    third, last_direction, out = refs[9:]
    squares = sum(ref[0:1, :] for ref in squares)
    length = jnp.sqrt(to_column(squares) + EPSILON)
    model_lens = [ref[:, 0:1] for ref in model_lens] + [length]
    steps, residual = scalars([ref[:, 0:1] for ref in data_lens], model_lens)
    for t in range(4):
        model = third[:, 1024 * t : 1024 * t + 1024].astype(F32) / length
        out[t] = model - steps[1][1] * last_direction[t]


def shift(value, step):
    return lax.ppermute(value, "x", [(i, (i + step) % 4) for i in range(4)])


def swap_core(value):
    return lax.ppermute(value, "c", [(0, 1), (1, 0)])


def exchange(value):
    width = value.shape[1]
    value = lax.all_to_all(
        value.reshape(32, 8, width), ("z", "y"), split_axis=0, concat_axis=0, tiled=True
    )
    return value.reshape(256, width)


PARTIAL = [((256, 640), F32), ((256, 640), BF)]
PARTIAL_SCRATCH = [((4, 512, 128), F32), ((10, 64, 128), BF)]
CHUNKS = [((208, 128), BF)] * 4
COLUMN = ((64, 128), F32)
MODEL = ((64, 4096), BF)


def on_device(left, right, observations):
    left = left.reshape(10, 128, 1024)
    right = right.reshape(10, 4, 32, 1024)
    observations = observations.reshape(10, 64, 1024)

    def sum_dp(whole, extra, before_gather=()):
        state, send = call(
            functools.partial(shard_kernel, not extra),
            [((16, 512), F32), ((256, 512), BF)],
            name="shard",
        )(exchange(whole), *extra)
        mine = exchange(send)
        if before_gather:
            mine = hold(mine, (), before_gather)
        return state, mine, swap_core(mine)

    one, two, three = call(pack_kernel, [((5, 128, 512), BF)] * 3, name="pack")(left)
    slots, squares, own_field = call(
        start_kernel,
        [((10, 64, 128), BF), ((8, 128), F32), ((5, 64, 512), BF)],
        name="start",
        after=(one, two, three),
    )(left, observations)
    keep, send = call(first_back_kernel, PARTIAL, PARTIAL_SCRATCH[:1], name="start_sum")(
        right, slots, squares
    )
    one, three = shift(one, 1), shift(three, 3)
    two = shift(hold(two, (right,), (one, three)), 2)
    blocks = [one, two, three]
    whole = call(core_kernel, [((256, 640), BF)], name="core_sum")(
        keep, swap_core(send)
    )[0]
    state, mine, other = sum_dp(whole, (), (two,))
    one, *blocks = blocks
    blocks = call(
        fetch_kernel,
        [((5, 128, 512), BF)] * 2,
        [pltpu.SemaphoreType.DMA((2,))],
        name="fetch",
        after=(mine,),
        anywhere=True,
    )(*blocks)
    field, factors = own_field, (left, one, *blocks)
    models, model_lens, data_lens = [], [], []
    for sweep in range(ITERS):
        model, *chunks = call(
            forward_kernel,
            [MODEL] + CHUNKS,
            [((4, 512, 128), F32), ((10, 64, 128), BF)],
            name="forward",
            after=tuple(blocks) if sweep == 0 else (),
        )(mine, other, right)
        models.append(model)
        chunks = [chunks[0]] + [shift(chunks[step], step) for step in (1, 2, 3)]
        last = sweep == ITERS - 1
        outs = call(
            functools.partial(data_kernel, last),
            [COLUMN, COLUMN]
            + CHUNKS
            + ([] if last else [((5, 64, 512), F32), ((5, 512, 512), BF)]),
            name="data",
        )(*chunks, field, state, *factors)
        model_lens.append(outs[0])
        data_lens.append(outs[1])
        field, factors = (None, None) if last else (outs[6], outs[7:])
        chunks = [outs[2]] + [shift(outs[2 + step], -step) for step in (1, 2, 3)]
        keep, send = call(
            back_kernel, PARTIAL, PARTIAL_SCRATCH + [((4, 64, 128), F32)], name="back"
        )(right, *chunks)
        whole = call(core_kernel, [((256, 640), BF)], name="core_sum")(
            keep, swap_core(send)
        )[0]
        state, mine, other = sum_dp(whole, (state, model_lens[-1]))

    model, data_len, squares = call(
        last_model_kernel,
        [MODEL, COLUMN, ((8, 128), F32)],
        [((4, 512, 128), F32)],
        name="last_model",
    )(mine, other, state)
    data_lens.append(data_len)
    solve_after = (squares,)
    squares = [squares] + [shift(squares, step) for step in (1, 2, 3)]
    solved, residual, last_direction = call(
        solution_kernel,
        [((4, 64, 1024), F32), COLUMN, ((4, 64, 1024), F32)],
        name="solve",
        after=solve_after,
    )(*data_lens, *model_lens, *models)
    direction = call(direction_kernel, [((4, 64, 1024), F32)], name="direct")(
        *data_lens, *model_lens, *squares, model, last_direction
    )[0]
    return solved, direction, residual[:, 0]


def solution(mesh):
    fine = Mesh(mesh.devices.reshape(8, 4, 2, 4), ("z", "y", "c", "x"))
    rows = ("z", "y", "c")
    return jax.shard_map(
        on_device,
        mesh=fine,
        in_specs=(
            P(rows, None, "x", None, None),
            P(rows, None, "x", None, None),
            P(rows, None, None, None),
        ),
        out_specs=(P("x", None, None), P("x", None, None), P()),
        check_vma=False,
    )
```

```python
import functools

import jax
import jax.numpy as jnp
from jax import lax
from jax.experimental import pallas as pl
from jax.experimental.pallas import tpu as pltpu
from jax.sharding import Mesh
from jax.sharding import PartitionSpec as P

ITERS = 2
EPSILON = 1e-06
BF = jnp.bfloat16
F32 = jnp.float32
VMEM_LIMIT = 20 * 1024 * 1024


def call(kernel, outs, scratch=(), name=None, after=(), anywhere=False, out_space=pltpu.VMEM):
    given = kernel

    def run(*operands):
        count = len(operands)

        def kernel(*refs):
            core = lax.axis_index("c")
            row = 32 * core + 4 * lax.axis_index("z") + lax.axis_index("y")
            places = (lax.axis_index("x"), core, row)
            given(places, *refs[:count], *refs[count + len(after) :])

        return pl.pallas_call(
            kernel,
            out_shape=[jax.ShapeDtypeStruct(out[0], out[1]) for out in outs],
            in_specs=[pl.BlockSpec(memory_space=pl.ANY if anywhere else pltpu.VMEM)]
            * len(operands)
            + [pl.BlockSpec(memory_space=pl.ANY)] * len(after),
            out_specs=[pl.BlockSpec(memory_space=out_space)] * len(outs),
            scratch_shapes=[
                pltpu.VMEM(*entry) if isinstance(entry, tuple) else entry
                for entry in scratch
            ],
            compiler_params=pltpu.CompilerParams(vmem_limit_bytes=VMEM_LIMIT),
            name=name,
        )(*operands, *after)

    return run


def dot(first, second):
    return jnp.dot(first, second, preferred_element_type=F32)


def dot_nt(first, second):
    return lax.dot_general(
        first, second, (((1,), (1,)), ((), ())), preferred_element_type=F32
    )


def split(value):
    first = value.astype(BF).astype(F32)
    rest = value - first
    second = rest.astype(BF).astype(F32)
    return first, second, (rest - second).astype(BF).astype(F32)


def lane_sum(value):
    return jnp.sum(value, axis=-1, keepdims=True)


def pieces_in_rows(row, count=8):
    first, second, third = split(row)
    at = lax.broadcasted_iota(jnp.int32, (count, 128), 0)
    return jnp.where(
        at == 0, first, jnp.where(at == 1, second, jnp.where(at == 2, third, 0.0))
    )


def part(index):
    return pl.ds(64 * index, 64)


TAIL = pl.ds(192, 16)


def squares_of(chunks):
    total = sum(chunk[TAIL, :].astype(F32) for chunk in chunks)
    return jnp.sum(total, axis=0, keepdims=True)


def diagonal():
    return lax.broadcasted_iota(jnp.int32, (64, 128), 0) == lax.broadcasted_iota(
        jnp.int32, (64, 128), 1
    )


def to_row(column):
    return jnp.sum(jnp.where(diagonal(), column, 0.0), axis=0, keepdims=True)


def to_column(row):
    return lane_sum(jnp.where(diagonal(), row, 0.0))


def write_partial(places, coeffs, right, squares, keep, send, field):
    for t in range(4):
        factors = jnp.concatenate([right[pair, t] for pair in range(10)], axis=0)
        value = dot(coeffs(t), factors)
        for i in range(8):
            field[i % 4, pl.ds(2 * t + i // 4, 64, stride=8), :] = value[
                :, 128 * i : 128 * i + 128
            ]
    core = places[1]
    kept = pl.ds(pl.multiple_of(256 * core, 256), 256)
    sent = pl.ds(pl.multiple_of(256 * (1 - core), 256), 256)
    for i in range(4):
        keep[:, 128 * i : 128 * i + 128] = field[i, kept, :]
        send[:, 128 * i : 128 * i + 128] = field[i, sent, :].astype(BF)
    tail = jnp.concatenate([pieces_in_rows(squares)] * 32, axis=0)
    keep[:, 512:640] = tail
    send[:, 512:640] = tail.astype(BF)


def in_slots(slots):
    return lambda t: jnp.concatenate(
        [slots[j][:, 32 * t : 32 * t + 32] for j in range(10)], axis=1
    )


def start_kernel(places, left, observations, slots, squares, own_field):
    for unit in range(5):
        own_field[unit] = unit_of(observations, places[0], unit)
    total = jnp.zeros((64, 128), F32)
    for pair in range(10):
        values = observations[pair]
        wide = values.astype(F32)
        wide = wide * wide
        total = total + sum(wide[:, 128 * i : 128 * i + 128] for i in range(8))
        slots[pair] = dot_nt(values, left[pair]).astype(BF)
    squares[...] = jnp.broadcast_to(to_row(lane_sum(total)), (8, 128))


def first_back_kernel(places, right, slots, squares, keep, send, field):
    write_partial(places, in_slots(slots), right, squares[0:1, :], keep, send, field)


def pack_kernel(places, left, one, two, three):
    here = places[0]
    for unit in range(5):
        for step, out in ((1, one), (2, two), (3, three)):
            out[unit] = unit_of(left, lax.rem(here + step, 4), unit)


def hold(value, kept=(), after=()):
    return pl.pallas_call(
        lambda *refs: None,
        out_shape=jax.ShapeDtypeStruct(value.shape, value.dtype),
        in_specs=[pl.BlockSpec(memory_space=pl.ANY)]
        + [pl.BlockSpec(memory_space=pltpu.VMEM)] * len(kept)
        + [pl.BlockSpec(memory_space=pl.ANY)] * len(after),
        out_specs=pl.BlockSpec(memory_space=pl.ANY),
        input_output_aliases={0: 0},
        compiler_params=pltpu.CompilerParams(vmem_limit_bytes=VMEM_LIMIT),
        name="hold",
    )(value, *kept, *after)


def unit_of(ref, owner, unit):
    if unit < 4:
        return ref[2 * owner + unit // 2, :, 512 * (unit % 2) : 512 * (unit % 2) + 512]
    half = pl.ds(pl.multiple_of(512 * lax.rem(owner, 2), 512), 512)
    return ref[8 + owner // 2, :, half]


def back_kernel(places, right, own, one, two, three, keep, send, field, slots, shared):
    here = places[0]
    chunks = (own, one, two, three)
    squares = squares_of(chunks)
    for step, chunk in enumerate(chunks):
        peer = lax.rem(here + step, 4)
        slots[2 * peer] = chunk[part(0), :]
        slots[2 * peer + 1] = chunk[part(1), :]
        shared[peer] = chunk[part(2), :].astype(F32)
    slots[8] = (shared[0] + shared[1]).astype(BF)
    slots[9] = (shared[2] + shared[3]).astype(BF)
    write_partial(places, in_slots(slots), right, squares, keep, send, field)


def core_kernel(places, keep, got, out):
    both = keep[...] + got[...].astype(F32)
    out[:, 0:512] = both[:, 0:512].astype(BF)
    tail = pieces_in_rows(jnp.sum(both[0:8, 512:640], axis=0, keepdims=True))
    out[:, 512:640] = jnp.concatenate([tail] * 32, axis=0).astype(BF)


def shard_kernel(first, places, got, *refs):
    before, model_len = (None, None) if first else refs[:2]
    state, send = refs[0 if first else 2 :]
    total = jnp.sum(got[...].astype(F32).reshape(32, 8, 640), axis=0)
    squares = jnp.sum(total[:, 512:640], axis=0, keepdims=True)
    data_len = jnp.sqrt(squares + EPSILON)
    row = places[2]
    at = lax.broadcasted_iota(jnp.int32, (1, 128), 1)
    length = lane_sum(jnp.where(at == row, data_len, 0.0))
    value = total[:, 0:512] / length
    if not first:
        ratio = length / model_len[pl.ds(row, 1), 0:1]
        value = value - ratio * before[0:8, :]
    state[0:8, :] = value
    state[8:16, 0:128] = jnp.broadcast_to(data_len, (8, 128))
    state[8:16, 128:512] = jnp.zeros((8, 384), F32)
    send[...] = jnp.concatenate([value] * 32, axis=0).astype(BF)


def first_shard_kernel(places, got, state, send, state_here, send_here, sems):
    shard_kernel(True, places, got, state_here, send_here)
    copies = [
        pltpu.make_async_copy(send_here, send, sems.at[0]),
        pltpu.make_async_copy(state_here, state, sems.at[1]),
    ]
    for copy in copies:
        copy.start()
    for copy in copies:
        copy.wait()


def length_column(state):
    return jnp.broadcast_to(to_column(state[8:9, 0:128]), (64, 128))


def read_model(places, mine, other, model, field):
    core = places[1]
    here = pl.ds(pl.multiple_of(256 * core, 256), 256)
    there = pl.ds(pl.multiple_of(256 * (1 - core), 256), 256)
    for i in range(4):
        field[i, here, :] = mine[:, 128 * i : 128 * i + 128].astype(F32)
        field[i, there, :] = other[:, 128 * i : 128 * i + 128].astype(F32)
    total = jnp.zeros((64, 128), F32)
    for at in range(32):
        value = field[at % 4, pl.ds(at // 4, 64, stride=8), :]
        model[:, 128 * at : 128 * at + 128] = value.astype(BF)
        total = total + value * value
    return lane_sum(total)


def forward_kernel(places, mine, other, right, model, own, one, two, three, field, slots):
    squares = read_model(places, mine, other, model, field)
    for t in range(4):
        factors = jnp.concatenate([right[pair, t] for pair in range(10)], axis=0)
        value = dot_nt(model[:, 1024 * t : 1024 * t + 1024], factors).astype(BF)
        for j in range(10):
            slots[j, :, 32 * t : 32 * t + 32] = value[:, 32 * j : 32 * j + 32]
    tail = pieces_in_rows(to_row(squares), 16).astype(BF)
    here = places[0]
    for step, chunk in enumerate((own, one, two, three)):
        peer = lax.rem(here + step, 4)
        chunk[part(0), :] = slots[2 * peer]
        chunk[part(1), :] = slots[2 * peer + 1]
        chunk[part(2), :] = slots[8 + peer // 2]
        chunk[TAIL, :] = tail


def fetch_kernel(places, two, three, two_here, three_here, sems):
    copies = [
        pltpu.make_async_copy(source, target, sems.at[at])
        for at, (source, target) in enumerate(((two, two_here), (three, three_here)))
    ]
    for copy in copies:
        copy.start()
    for copy in copies:
        copy.wait()


def data_kernel(last, places, *refs):
    coeffs, refs = refs[:4], refs[4:]
    (field, state, units), refs = (refs[:3], refs[3:]) if last else ((*refs[:2], refs[-1]), refs[2:])
    if not last:
        blocks, refs = refs[:4], refs[4:]
        for unit in range(5):
            units[unit, 0:128, :] = unit_of(blocks[0], places[0], unit)
            for step in (1, 2, 3):
                units[unit, 128 * step : 128 * step + 128, :] = blocks[step][unit]
    model_len, data_len, outs = refs[0], refs[1], refs[2:6]
    data_len[...] = length_column(state)
    length = to_column(jnp.sqrt(squares_of(coeffs) + EPSILON))
    model_len[...] = jnp.broadcast_to(length, (64, 128))
    inverse = 1.0 / length
    ratio = length / data_len[:, 0:1]
    total = jnp.zeros((64, 128), F32)
    for i in range(3):
        given = jnp.concatenate([chunk[part(i), :] for chunk in coeffs], axis=1)
        back = None
        for unit in range(2 * i, min(2 * i + 2, 5)):
            factors = units[unit]
            value = dot(given, factors) * inverse - ratio * field[unit].astype(F32)
            if not last:
                refs[6][unit] = value
            term = dot_nt(value.astype(BF), factors)
            back = term if back is None else back + term
            value = value * value
            total = total + sum(value[:, 128 * k : 128 * k + 128] for k in range(4))
        back = back.astype(BF)
        for step in range(4):
            outs[step][part(i), :] = back[:, 128 * step : 128 * step + 128]
    tail = pieces_in_rows(to_row(lane_sum(total)), 16).astype(BF)
    for step in range(4):
        outs[step][TAIL, :] = tail


def last_model_kernel(places, mine, other, state, model, data_len, squares, field):
    data_len[...] = length_column(state)
    total = to_row(read_model(places, mine, other, model, field))
    squares[...] = jnp.broadcast_to(total, (8, 128))


def scalars(data_lens, model_lens):
    diagonal_bar, residual = model_lens[0], data_lens[0]
    out = []
    for sweep in range(ITERS):
        data_len = data_lens[sweep + 1]
        rotation = jnp.sqrt(diagonal_bar * diagonal_bar + data_len * data_len)
        cosine_term = diagonal_bar / rotation
        sine_term = data_len / rotation
        into_solution = (cosine_term * residual) / rotation
        residual = sine_term * residual
        into_direction = None
        if sweep + 1 < len(model_lens):
            into_direction = (sine_term * model_lens[sweep + 1]) / rotation
            diagonal_bar = -cosine_term * model_lens[sweep + 1]
        out.append((into_solution, into_direction))
    return out, residual


def solution_kernel(places, *refs):
    data_lens, model_lens, (first, second) = refs[:3], refs[3:5], refs[5:7]
    solved, residual_estimate, last_direction = refs[7:]
    model_lens = [ref[:, 0:1] for ref in model_lens]
    steps, residual = scalars([ref[:, 0:1] for ref in data_lens], model_lens)
    residual_estimate[...] = jnp.broadcast_to(residual, (64, 128))
    for t in range(4):
        part = slice(1024 * t, 1024 * t + 1024)
        direction = first[:, part].astype(F32) / model_lens[0]
        value = steps[0][0] * direction
        direction = second[:, part].astype(F32) / model_lens[1] - steps[0][1] * direction
        solved[t] = value + steps[1][0] * direction
        last_direction[t] = direction


def direction_kernel(places, *refs):
    data_lens, model_lens, squares = refs[:3], refs[3:5], refs[5:9]
    third, last_direction, out = refs[9:]
    squares = sum(ref[0:1, :] for ref in squares)
    length = jnp.sqrt(to_column(squares) + EPSILON)
    model_lens = [ref[:, 0:1] for ref in model_lens] + [length]
    steps, residual = scalars([ref[:, 0:1] for ref in data_lens], model_lens)
    for t in range(4):
        model = third[:, 1024 * t : 1024 * t + 1024].astype(F32) / length
        out[t] = model - steps[1][1] * last_direction[t]


def shift(value, step):
    return lax.ppermute(value, "x", [(i, (i + step) % 4) for i in range(4)])


def swap_core(value):
    return lax.ppermute(value, "c", [(0, 1), (1, 0)])


def exchange(value):
    width = value.shape[1]
    value = lax.all_to_all(
        value.reshape(32, 8, width), ("z", "y"), split_axis=0, concat_axis=0, tiled=True
    )
    return value.reshape(256, width)


PARTIAL = [((256, 640), F32), ((256, 640), BF)]
PARTIAL_SCRATCH = [((4, 512, 128), F32), ((10, 64, 128), BF)]
CHUNKS = [((208, 128), BF)] * 4
COLUMN = ((64, 128), F32)
MODEL = ((64, 4096), BF)


def on_device(left, right, observations):
    left = left.reshape(10, 128, 1024)
    right = right.reshape(10, 4, 32, 1024)
    observations = observations.reshape(10, 64, 1024)

    def sum_dp(whole, extra, before_gather=()):
        shard = [((16, 512), F32), ((256, 512), BF)]
        if extra:
            kernel, scratch, space = functools.partial(shard_kernel, False), [], pltpu.VMEM
        else:
            kernel, space = first_shard_kernel, pltpu.HBM
            scratch = shard + [pltpu.SemaphoreType.DMA((2,))]
        state, send = call(kernel, shard, scratch, name="shard", out_space=space)(
            exchange(whole), *extra
        )
        mine = exchange(send)
        if before_gather:
            mine = hold(mine, (), before_gather)
        return state, mine, swap_core(mine)

    one, two, three = call(pack_kernel, [((5, 128, 512), BF)] * 3, name="pack")(left)
    slots, squares, own_field = call(
        start_kernel,
        [((10, 64, 128), BF), ((8, 128), F32), ((5, 64, 512), BF)],
        name="start",
        after=(one, two, three),
    )(left, observations)
    keep, send = call(first_back_kernel, PARTIAL, PARTIAL_SCRATCH[:1], name="start_sum")(
        right, slots, squares
    )
    one, three = shift(one, 1), shift(three, 3)
    two = shift(hold(two, (right,), (one, three)), 2)
    blocks = [one, two, three]
    whole = call(core_kernel, [((256, 640), BF)], name="core_sum")(
        keep, swap_core(send)
    )[0]
    state, mine, other = sum_dp(whole, (), (two,))
    one, *blocks = blocks
    blocks = call(
        fetch_kernel,
        [((5, 128, 512), BF)] * 2,
        [pltpu.SemaphoreType.DMA((2,))],
        name="fetch",
        after=(mine,),
        anywhere=True,
    )(*blocks)
    field, factors = own_field, (left, one, *blocks)
    models, model_lens, data_lens = [], [], []
    for sweep in range(ITERS):
        model, *chunks = call(
            forward_kernel,
            [MODEL] + CHUNKS,
            [((4, 512, 128), F32), ((10, 64, 128), BF)],
            name="forward",
            after=tuple(blocks) if sweep == 0 else (),
        )(mine, other, right)
        models.append(model)
        chunks = [chunks[0]] + [shift(chunks[step], step) for step in (1, 2, 3)]
        last = sweep == ITERS - 1
        outs = call(
            functools.partial(data_kernel, last),
            [COLUMN, COLUMN]
            + CHUNKS
            + ([] if last else [((5, 64, 512), F32), ((5, 512, 512), BF)]),
            name="data",
        )(*chunks, field, state, *factors)
        model_lens.append(outs[0])
        data_lens.append(outs[1])
        field, factors = (None, None) if last else (outs[6], outs[7:])
        chunks = [outs[2]] + [shift(outs[2 + step], -step) for step in (1, 2, 3)]
        keep, send = call(
            back_kernel, PARTIAL, PARTIAL_SCRATCH + [((4, 64, 128), F32)], name="back"
        )(right, *chunks)
        whole = call(core_kernel, [((256, 640), BF)], name="core_sum")(
            keep, swap_core(send)
        )[0]
        state, mine, other = sum_dp(whole, (state, model_lens[-1]))

    model, data_len, squares = call(
        last_model_kernel,
        [MODEL, COLUMN, ((8, 128), F32)],
        [((4, 512, 128), F32)],
        name="last_model",
    )(mine, other, state)
    data_lens.append(data_len)
    solve_after = (squares,)
    squares = [squares] + [shift(squares, step) for step in (1, 2, 3)]
    solved, residual, last_direction = call(
        solution_kernel,
        [((4, 64, 1024), F32), COLUMN, ((4, 64, 1024), F32)],
        name="solve",
        after=solve_after,
    )(*data_lens, *model_lens, *models)
    direction = call(direction_kernel, [((4, 64, 1024), F32)], name="direct")(
        *data_lens, *model_lens, *squares, model, last_direction
    )[0]
    return solved, direction, residual[:, 0]


def solution(mesh):
    fine = Mesh(mesh.devices.reshape(8, 4, 2, 4), ("z", "y", "c", "x"))
    rows = ("z", "y", "c")
    return jax.shard_map(
        on_device,
        mesh=fine,
        in_specs=(
            P(rows, None, "x", None, None),
            P(rows, None, "x", None, None),
            P(rows, None, None, None),
        ),
        out_specs=(P("x", None, None), P("x", None, None), P()),
        check_vma=False,
    )
```
